128 devices in a mesh: dp: 4 (over z), expert: 32 (over x, y, core).
Axes of the slice: x: 4, y: 4, z: 4, core: 2. Of those that a mesh axis runs over, the one named last changes fastest.
Arguments:
- layer_input: bfloat16 [16384, 2048], P(('dp', 'expert')), may hold values from -42 to 42
- upstream: bfloat16 [16384, 2048], P(('dp', 'expert')), may hold values from -1.5 to 1.5
- hidden: bfloat16 [16384, 8, 768], P(('dp', 'expert')), may hold values from -6 to 6
- route_ids: int32 [16384, 8], P(('dp', 'expert')), may hold values from 0 to 95, all different within a row; in each aligned block of 128 rows (0 to 127, 128 to 255, ...) at most 16 rows name the same one
- route_prob: float32 [16384, 8], P(('dp', 'expert')), may hold values from 0.05 to 1
- down_weight: bfloat16 [96, 768, 2048], P('expert'), may hold values from -0.21875 to 0.21875
- probe_signs: bfloat16 [96, 768, 2048], P('expert'), may hold values from -1 to 1, as said below
Outputs:
- diag_estimate: float32 [96, 768, 2048], P('expert', None, 'dp')
The draws below stay inside these ranges and needn't reach their ends.
Inputs may be any that keep to these rules, and one draw needn't show every extreme that they name: `route_ids`: each row names 8 different experts. Among the 128 rows of one device (aligned blocks of rows) no expert is named by more than 16 rows, and in every draw some expert is named by exactly 16 rows of one device. `probe_signs`: every entry is -1 or +1.
All inputs are finite; a program needn't handle non-finite values.
Results may differ from the reference program's by a relative error of at most 0.0045.
Values may be sent and summed in bfloat16 or wider, within the bound.
No kernel may reach another device: no remote copies, remote signals or barrier semaphores. Data moves between devices by JAX's collectives and lax.ppermute only.
A program may use at most 192 MiB of HBM per device.

```python
import math
import jax
import jax.numpy as jnp
import numpy as np
from jax import lax

D = 2048
F = 768
TOPK = 8
TOK_DEV = 128
EXPERTS = 96
CAP = 16
TOKENS = 16384
N_DP = 4
N_EXPERT = 32


def draw_layer_input(key, part):
    key = jax.random.fold_in(key, 5)
    key_rows, key_cols, key_values = jax.random.split(key, 3)
    row_scale = jnp.exp(jax.random.uniform(key_rows, (TOKENS, 1), jnp.float32, 0.0, math.log(10.0)))
    col_scale = jnp.exp(jax.random.uniform(key_cols, (1, D), jnp.float32, 0.0, math.log(10.0)))
    values = jnp.clip(jax.random.normal(key_values, (TOKENS, D), jnp.float32), -4.0, 4.0)
    return (values * row_scale * col_scale * 0.1).astype(jnp.bfloat16)


def draw_probe_signs(key, part):
    key = jax.random.fold_in(key, 9)
    sign_bits = jax.random.randint(key, (EXPERTS, F, D), 0, 2)
    return (2.0 * sign_bits.astype(jnp.float32) - 1.0).astype(jnp.bfloat16)


def block_levels(rng, extent, cuts, low, largest):
    level = 1.0
    for dim, parts in cuts:
        steps = jax.random.uniform(jax.random.fold_in(jax.random.fold_in(rng, 6), dim), (parts,), jnp.float32, low / len(cuts), largest / len(cuts))
        level = level * jnp.repeat(jnp.exp(steps), extent[dim] // parts).reshape((-1,) + (1,) * (len(extent) - 1 - dim))
    return level


def routed_block(stream_key, own, number, rows, amount, top, reach, slope):
    ranking = jax.random.permutation(stream_key, amount)
    packed, usual = portions_of(amount, rows * top, reach, slope, True), portions_of(amount, rows * top, reach, slope, False)
    places = jnp.arange(amount)

    def named(lengths, turn):
        used = int((lengths > 0).sum())
        fixed = max(1, used // 4)
        passed = fixed + (places - fixed + turn * (used - fixed)) % max(1, amount - fixed)
        return jnp.zeros((amount,), jnp.int32).at[ranking[jnp.where(places < fixed, places, passed)]].set(jnp.asarray(lengths, jnp.int32))

    lengths = jnp.where(number % 4 == 0, named(packed, number // 4), named(usual, number - number // 4 - 1))
    mixed = jax.random.permutation(jax.random.fold_in(own, 3), amount)
    giver, taker = mixed[0:amount // 2 * 2:2], mixed[1:amount // 2 * 2:2]
    room = jnp.minimum(lengths[giver] - 1, reach - lengths[taker]) // 2
    room = jnp.where((giver == ranking[0]) | (taker == ranking[0]) | (lengths[taker] == 0), 0, jnp.maximum(room, 0))
    passed = jax.random.randint(jax.random.fold_in(own, 4), (amount // 2,), 0, 1 << 20) % (room + 1)
    lengths = lengths.at[giver].add(-passed).at[taker].add(passed)
    items = jnp.searchsorted(jnp.cumsum(lengths), jnp.arange(rows * top), side="right").astype(jnp.int32)
    listing = items.reshape(top, rows).T
    listing = listing[jax.random.permutation(jax.random.fold_in(own, 1), rows)]
    turn = jax.random.randint(jax.random.fold_in(own, 2), (rows, 1), 0, top)
    return jnp.take_along_axis(listing, (jnp.arange(top)[None, :] + turn) % top, axis=1)


def portions_of(count, total, most, lean, full):
    loads = [(1 << 20) // math.isqrt(rank ** lean) + 1 for rank in range(1, count + 1)]
    largest = most if full else min(most, max(-(-total // count), total * loads[0] // sum(loads)))
    least = 1 if total - largest >= count - 1 else 0
    counts, spare = [largest] + [least] * (count - 1), total - largest - least * (count - 1)
    while spare > 0:
        candidates = [i for i in range(1, count) if counts[i] < largest] or [i for i in range(1, count) if counts[i] < most]
        whole, budget = sum([loads[i] for i in candidates]), spare
        for i in candidates:
            extra = min(most - counts[i], max(1, budget * loads[i] // whole), spare)
            counts[i] = counts[i] + extra
            spare = spare - extra
    return np.array(counts)


def gaussian(stream_key, extent, scale, most, shards=(), kind=jnp.bfloat16):
    result = scale * jax.random.normal(stream_key, extent, jnp.float32)
    if shards:
        result = result * block_levels(stream_key, extent, shards, -0.22, 0.18)
    return jnp.clip(result, -most, most).astype(kind)


def setup_inputs(seed: int = 0) -> dict:
    streams_of = jax.random.split(jax.random.key(seed), 8)
    layer_input = draw_layer_input(jax.random.fold_in(streams_of[7], 71), 0)
    upstream = gaussian(streams_of[1], (TOKENS, D), 0.25, 1.5, ((0, 128),))
    hidden = gaussian(streams_of[2], (TOKENS, TOPK, F), 1.0, 6.0, ((0, 128),))
    route_ids_keys = jax.random.split(jax.random.fold_in(streams_of[3], 1), TOKENS // TOK_DEV)
    route_ids_turns = jax.random.permutation(jax.random.fold_in(streams_of[3], 3), TOKENS // TOK_DEV)
    route_ids = jax.vmap(lambda own, number: routed_block(jax.random.fold_in(streams_of[3], 2), own, number, TOK_DEV, EXPERTS, TOPK, CAP, 2))(route_ids_keys, route_ids_turns).reshape((TOKENS, TOPK))
    route_prob = jnp.clip(jnp.exp(math.log(1.0) - 2.9957323 * jax.random.uniform(streams_of[4], (TOKENS, TOPK), jnp.float32) ** block_levels(streams_of[4], (TOKENS, TOPK), ((0, 128),), -0.2, 0.2)), 0.05, 1.0)
    down_weight = gaussian(streams_of[5], (EXPERTS, F, D), F ** -0.5, 0.21875, ((0, 32),))
    probe_signs = draw_probe_signs(jax.random.fold_in(streams_of[7], 71), 0)
    return dict(layer_input=layer_input, upstream=upstream, hidden=hidden, route_ids=route_ids, route_prob=route_prob, down_weight=down_weight, probe_signs=probe_signs)


EPSILON = 1e-06

def curvature_tangent(layer_input, upstream, moe_out, moe_tangent):
    summed = layer_input.astype(jnp.float32) + moe_out
    coefficient = upstream.astype(jnp.float32)
    inverse = lax.rsqrt(lax.optimization_barrier(jnp.mean(summed * summed, axis=-1, keepdims=True)) + EPSILON)
    inverse_cube = inverse * inverse * inverse
    upstream_dot = lax.optimization_barrier(jnp.mean(coefficient * summed, axis=-1, keepdims=True))
    stretch = lax.optimization_barrier(jnp.mean(summed * moe_tangent, axis=-1, keepdims=True))
    turning = lax.optimization_barrier(jnp.mean(coefficient * moe_tangent, axis=-1, keepdims=True))
    first = -inverse_cube * stretch * coefficient
    second = (3.0 * inverse_cube * inverse * inverse * stretch * upstream_dot - inverse_cube * turning) * summed
    third = inverse_cube * upstream_dot * moe_tangent
    return first + second - third

def reference(layer_input, upstream, hidden, route_ids, route_prob, down_weight, probe_signs):
    devices = N_DP * N_EXPERT
    combine = route_prob / lax.optimization_barrier(jnp.sum(route_prob, axis=1, keepdims=True))
    grouped = route_ids.reshape(devices, TOK_DEV * TOPK)
    onehot = (grouped[:, :, None] == jnp.arange(EXPERTS, dtype=jnp.int32)[None, None, :]).astype(jnp.int32)
    earlier = lax.optimization_barrier(jnp.sum((jnp.cumsum(onehot, axis=1) - onehot) * onehot, axis=2))
    source = jnp.arange(devices, dtype=jnp.int32)[:, None]
    placing = (grouped * (devices * CAP) + source * CAP + earlier).reshape(-1).astype(jnp.int32)
    slots_all = EXPERTS * devices * CAP
    owner_ids = (jnp.arange(TOKENS * TOPK, dtype=jnp.int32) // TOPK).astype(jnp.int32)
    buffer = jnp.zeros((slots_all, F), jnp.bfloat16).at[placing].set(hidden.reshape(-1, F))
    buffer = buffer.reshape(EXPERTS, devices * CAP, F)
    weights_buf = jnp.zeros((slots_all,), jnp.float32).at[placing].set(combine.reshape(-1))
    weights_buf = weights_buf.reshape(EXPERTS, devices * CAP)
    owners_buf = jnp.full((slots_all,), TOKENS, jnp.int32).at[placing].set(owner_ids)
    owners_buf = owners_buf.reshape(EXPERTS, devices * CAP)

    def forward_step(running, inputs):
        slot_rows, down_mat, probe_mat, slot_weights, slot_owner = inputs
        primal = jnp.dot(slot_rows, down_mat, preferred_element_type=jnp.float32).astype(jnp.bfloat16)
        tangent = jnp.dot(slot_rows, probe_mat, preferred_element_type=jnp.float32).astype(jnp.bfloat16)
        moe_out = running[0].at[slot_owner].add(slot_weights[:, None] * primal.astype(jnp.float32), mode='drop')
        moe_tangent = running[1].at[slot_owner].add(slot_weights[:, None] * tangent.astype(jnp.float32), mode='drop')
        return ((moe_out, moe_tangent), None)
    initial = (jnp.zeros((TOKENS, D), jnp.float32), jnp.zeros((TOKENS, D), jnp.float32))
    totals, ignored = lax.scan(forward_step, initial, (buffer, down_weight, probe_signs, weights_buf, owners_buf))
    grad_tangent = curvature_tangent(layer_input, upstream, totals[0], totals[1])
    padded = jnp.concatenate([grad_tangent, jnp.zeros((1, D), jnp.float32)], axis=0)

    def expert_estimate(inputs):
        slot_rows, probe_mat, slot_weights, slot_owner = inputs
        slot_grads = (slot_weights[:, None] * padded[slot_owner]).astype(jnp.bfloat16)
        curvature = jnp.dot(slot_rows.T, slot_grads, preferred_element_type=jnp.float32)
        return probe_mat.astype(jnp.float32) * curvature
    return lax.map(expert_estimate, (buffer, probe_signs, weights_buf, owners_buf))
```

```python
import jax
import jax.numpy as jnp
from jax import lax
from jax.experimental import pallas as pl
from jax.experimental.pallas import tpu as pltpu
from jax.sharding import PartitionSpec as P

EPSILON = 1e-06
CAP = 16
VMEM_LIMIT = 56 * 1024 * 1024
F32 = jnp.float32
BF16 = jnp.bfloat16


def params():
    return pltpu.CompilerParams(vmem_limit_bytes=VMEM_LIMIT)


def dot(a, b, dims):
    return lax.dot_general(a, b, (dims, ((), ())), preferred_element_type=F32)


def split_high_low(x):
    high = x.astype(BF16)
    low = (x - high.astype(F32)).astype(BF16)
    return high, low


def place_kernel(ids_ref, comb_ref, hidden_ref, out_ref, sel_ref):
    experts = out_ref.shape[0] // CAP
    routes, tokens = hidden_ref.shape[0], sel_ref.shape[0] // 2
    top = routes // tokens
    ids = ids_ref[...]
    named = lax.broadcasted_iota(jnp.int32, (experts, routes), 0) == ids
    named_f = named.astype(F32)
    before = lax.broadcasted_iota(jnp.int32, (routes, routes), 0) < lax.broadcasted_iota(
        jnp.int32, (routes, routes), 1
    )
    earlier = dot(named_f.astype(BF16), before.astype(F32).astype(BF16), ((1,), (0,)))
    rank = jnp.sum(named_f * earlier, axis=0, keepdims=True)
    place = ids * CAP + rank.astype(jnp.int32)
    owner = lax.broadcasted_iota(jnp.int32, (tokens, routes), 1) // top
    own = owner == lax.broadcasted_iota(jnp.int32, (tokens, routes), 0)
    weights = jnp.where(own, comb_ref[...], 0.0)
    high, low = split_high_low(weights)
    weights = jnp.concatenate([high, low], axis=0)
    hidden = hidden_ref[...]
    step = 512
    for first in range(0, experts * CAP, step):
        slots = lax.broadcasted_iota(jnp.int32, (step, routes), 0) + first
        pick = (slots == place).astype(F32).astype(BF16)
        out_ref[first : first + step, :] = dot(pick, hidden, ((1,), (0,))).astype(BF16)
        sel_ref[:, first : first + step] = dot(weights, pick, ((1,), (1,))).astype(BF16)


def place_routes(ids_row, comb_row, hidden, tokens, experts):
    return pl.pallas_call(
        place_kernel,
        out_shape=(
            jax.ShapeDtypeStruct((experts * CAP, hidden.shape[1]), BF16),
            jax.ShapeDtypeStruct((2 * tokens, experts * CAP), BF16),
        ),
        compiler_params=params(),
    )(ids_row, comb_row, hidden)


def rows_kernel(x_ref, w_ref, out_ref):
    groups, cap, width = x_ref.shape
    x = x_ref[...].reshape(groups * cap, width)
    rows = dot(x, w_ref[0], ((1,), (0,)))
    out_ref[...] = rows.astype(BF16).reshape(groups, cap, -1)


def expert_rows(arrived, weight):
    groups, slots, width_f = arrived.shape
    local, _, width_d = weight.shape
    tile = width_d // 2
    return pl.pallas_call(
        rows_kernel,
        grid=(local, width_d // tile),
        in_specs=[
            pl.BlockSpec((groups, CAP, width_f), lambda l, n: (0, l, 0)),
            pl.BlockSpec((1, width_f, tile), lambda l, n: (l, 0, n)),
        ],
        out_specs=pl.BlockSpec((groups, CAP, tile), lambda l, n: (0, l, n)),
        out_shape=jax.ShapeDtypeStruct((groups, slots, width_d), BF16),
        cost_estimate=pl.CostEstimate(
            flops=2 * groups * slots * width_f * width_d,
            bytes_accessed=2 * (weight.size + arrived.size + groups * slots * width_d),
            transcendentals=0,
        ),
        compiler_params=params(),
    )(arrived, weight)


def token_kernel(sel_ref, primal_ref, tangent_ref, li_ref, up_ref, out_ref, mo_s, mt_s):
    step = pl.program_id(0)
    tokens = li_ref.shape[0]
    tile = primal_ref.shape[1]
    quarters, _, quarter = out_ref.shape
    sel = sel_ref[...]
    mo = dot(sel, primal_ref[...], ((1,), (0,)))
    mt = dot(sel, tangent_ref[...], ((1,), (0,)))
    mo_s[step] = mo[:tokens] + mo[tokens:]
    mt_s[step] = mt[:tokens] + mt[tokens:]

    @pl.when(step == pl.num_programs(0) - 1)
    def _():
        steps = mo_s.shape[0]
        width = steps * tile
        sq = jnp.zeros((tokens, 1), F32)
        dot_us, dot_st, dot_ut = sq, sq, sq
        for n in range(steps):
            cols = slice(n * tile, (n + 1) * tile)
            summed = li_ref[:, cols].astype(F32) + mo_s[n]
            mo_s[n] = summed
            up = up_ref[:, cols].astype(F32)
            mt = mt_s[n]
            sq += jnp.sum(summed * summed, axis=1, keepdims=True)
            dot_us += jnp.sum(up * summed, axis=1, keepdims=True)
            dot_st += jnp.sum(summed * mt, axis=1, keepdims=True)
            dot_ut += jnp.sum(up * mt, axis=1, keepdims=True)
        inverse = lax.rsqrt(sq / width + EPSILON)
        cube = inverse * inverse * inverse
        a, s, u = dot_us / width, dot_st / width, dot_ut / width
        by_up = -cube * s
        by_summed = 3.0 * cube * inverse * inverse * s * a - cube * u
        by_mt = cube * a
        for n in range(steps):
            cols = slice(n * tile, (n + 1) * tile)
            up = up_ref[:, cols].astype(F32)
            grad = by_up * up + by_summed * mo_s[n] - by_mt * mt_s[n]
            part, offset = divmod(n * tile, quarter)
            out_ref[part, :, offset : offset + tile] = grad.astype(BF16)


def token_gradients(sel, primal, tangent, layer_input, upstream, quarters):
    tokens, width = layer_input.shape
    slots = primal.shape[0]
    tile = 256
    steps = width // tile
    return pl.pallas_call(
        token_kernel,
        grid=(steps,),
        in_specs=[
            pl.BlockSpec((2 * tokens, slots), lambda n: (0, 0)),
            pl.BlockSpec((slots, tile), lambda n: (0, n)),
            pl.BlockSpec((slots, tile), lambda n: (0, n)),
            pl.BlockSpec((tokens, width), lambda n: (0, 0)),
            pl.BlockSpec((tokens, width), lambda n: (0, 0)),
        ],
        out_specs=pl.BlockSpec((quarters, tokens, width // quarters), lambda n: (0, 0, 0)),
        out_shape=jax.ShapeDtypeStruct((quarters, tokens, width // quarters), BF16),
        scratch_shapes=[pltpu.VMEM((steps, tokens, tile), F32)] * 2,
        cost_estimate=pl.CostEstimate(
            flops=8 * tokens * slots * width, bytes_accessed=4 * slots * width, transcendentals=0
        ),
        compiler_params=params(),
    )(sel, primal, tangent, layer_input, upstream)


def estimate_kernel(rank_ref, comb_ref, hidden_ref, grad_ref, probe_ref, out_ref, rows_s):
    step = pl.program_id(0)
    groups = grad_ref.shape[0]
    tokens = grad_ref.shape[2]
    local = out_ref.shape[0]
    slot_iota = lax.broadcasted_iota(jnp.int32, (CAP, tokens), 0)

    def pick(i, carry):
        rank = rank_ref[0, i]
        comb = comb_ref[0, i]
        parts = [
            jnp.where(rank[l : l + 1, :] == slot_iota, comb[l : l + 1, :], 0.0) for l in range(local)
        ]
        high, low = split_high_low(jnp.concatenate(parts, axis=0))
        both = dot(jnp.concatenate([high, low], axis=0), grad_ref[i, 0], ((1,), (0,)))
        rows = (both[: local * CAP] + both[local * CAP :]).astype(BF16)
        for l in range(local):
            rows_s[l, pl.ds(pl.multiple_of(i * CAP, CAP), CAP), :] = rows[l * CAP : (l + 1) * CAP]
        return carry

    lax.fori_loop(0, groups, pick, 0, unroll=4)
    for l in range(local):
        hidden = hidden_ref[0, :, l * CAP : (l + 1) * CAP, :].reshape(groups * CAP, -1)
        part = dot(hidden, rows_s[l], ((0,), (0,)))

        @pl.when(step == 0)
        def _():
            out_ref[l] = part

        @pl.when(step > 0)
        def _():
            out_ref[l] += part

        @pl.when(step == pl.num_programs(0) - 1)
        def _():
            out_ref[l] = out_ref[l] * probe_ref[l].astype(F32)


def estimate(rank, comb, hidden, grads, probe):
    parts, groups, slots, width_f = hidden.shape
    tokens, quarter = grads.shape[2:]
    local = probe.shape[0]
    return pl.pallas_call(
        estimate_kernel,
        grid=(parts,),
        in_specs=[
            pl.BlockSpec((1, groups, local, tokens), lambda g: (g, 0, 0, 0)),
            pl.BlockSpec((1, groups, local, tokens), lambda g: (g, 0, 0, 0)),
            pl.BlockSpec((1, groups, slots, width_f), lambda g: (g, 0, 0, 0)),
            pl.BlockSpec((groups, 1, tokens, quarter), lambda g: (0, g, 0, 0)),
            pl.BlockSpec((local, width_f, quarter), lambda g: (0, 0, 0)),
        ],
        out_specs=pl.BlockSpec((local, width_f, quarter), lambda g: (0, 0, 0)),
        out_shape=jax.ShapeDtypeStruct((local, width_f, quarter), F32),
        scratch_shapes=[pltpu.VMEM((local, groups * CAP, quarter), BF16)],
        cost_estimate=pl.CostEstimate(
            flops=2 * parts * groups * slots * width_f * quarter,
            bytes_accessed=2 * (hidden.size + grads.size) + 6 * local * width_f * quarter,
            transcendentals=0,
        ),
        compiler_params=params(),
    )(rank, comb, hidden, grads, probe)


def local_routes(ids, comb, first, local):
    tokens = ids.shape[-1]
    own = first + jnp.arange(local, dtype=jnp.int32)
    match = ids[..., None, :, :] == own[:, None, None]
    named = jnp.any(match, axis=-2)
    weight = jnp.sum(jnp.where(match, comb[..., None, :, :], 0.0), axis=-2)
    before = jnp.triu(jnp.ones((tokens, tokens), F32), 1).astype(BF16)
    earlier = jnp.einsum(
        "gslt,tu->gslu", named.astype(BF16), before, preferred_element_type=F32
    ).astype(jnp.int32)
    return jnp.where(named, earlier, -1), weight


def shards(layer_input, upstream, hidden, route_ids, route_prob, down_weight, probe_signs):
    tokens, top = route_ids.shape
    local, width_f, width_d = down_weight.shape
    groups, parts = lax.axis_size("expert"), lax.axis_size("dp")
    experts = local * groups
    quarter = width_d // parts
    combine = route_prob / jnp.sum(route_prob, axis=1, keepdims=True)
    ids_t, comb_t = route_ids.T, combine.T
    outgoing, sel = place_routes(
        route_ids.reshape(1, -1), combine.reshape(1, -1), hidden.reshape(-1, width_f), tokens, experts
    )
    arrived = lax.all_to_all(
        outgoing.reshape(groups, local * CAP, width_f), "expert", 0, 0, tiled=True
    )
    ids_all = lax.all_gather(ids_t, ("dp", "expert"), axis=0, tiled=False)
    comb_all = lax.all_gather(comb_t, ("dp", "expert"), axis=0, tiled=False)
    hidden_all = lax.all_gather(arrived, "dp", axis=0, tiled=False)
    tangent = lax.all_to_all(expert_rows(arrived, probe_signs), "expert", 0, 0, tiled=True)
    primal = lax.all_to_all(expert_rows(arrived, down_weight), "expert", 0, 0, tiled=True)
    grads = token_gradients(
        sel,
        primal.reshape(-1, width_d),
        tangent.reshape(-1, width_d),
        layer_input,
        upstream,
        parts,
    )
    grads = lax.all_to_all(grads, "dp", 0, 0, tiled=True)
    grads_all = lax.all_gather(grads, "expert", axis=0, tiled=False)
    rank, comb = local_routes(
        ids_all.reshape(parts, groups, top, tokens),
        comb_all.reshape(parts, groups, top, tokens),
        lax.axis_index("expert") * local,
        local,
    )
    probe = lax.dynamic_slice_in_dim(probe_signs, lax.axis_index("dp") * quarter, quarter, 2)
    return estimate(rank, comb, hidden_all, grads_all, probe)


def solution(mesh):
    in_specs = (
        P(("dp", "expert"), None),
        P(("dp", "expert"), None),
        P(("dp", "expert"), None, None),
        P(("dp", "expert"), None),
        P(("dp", "expert"), None),
        P("expert", None, None),
        P("expert", None, None),
    )
    out_specs = P("expert", None, "dp")
    return jax.shard_map(shards, mesh=mesh, in_specs=in_specs, out_specs=out_specs, check_vma=False)
```

```python
import jax
import jax.numpy as jnp
from jax import lax
from jax.experimental import pallas as pl
from jax.experimental.pallas import tpu as pltpu
from jax.sharding import PartitionSpec as P

EPSILON = 1e-06
CAP = 16
SIDE = 4
CORES = 2
FACTS = 128
VMEM_LIMIT = 56 * 1024 * 1024
F32 = jnp.float32
BF16 = jnp.bfloat16


def params():
    return pltpu.CompilerParams(vmem_limit_bytes=VMEM_LIMIT)


def dot(a, b, dims):
    return lax.dot_general(a, b, (dims, ((), ())), preferred_element_type=F32)


def device_at(x, y, core):
    return (x * SIDE + y) * CORES + core


def shift(value, dx, dy, core):
    pairs = []
    for i in range(SIDE * SIDE * CORES):
        x, y, c = i // (SIDE * CORES), i // CORES % SIDE, i % CORES
        pairs.append((i, device_at((x + dx) % SIDE, (y + dy) % SIDE, c ^ core)))
    return lax.ppermute(value, "expert", pairs)


def place_kernel(ids_ref, hidden_ref, facts_ref, out_ref):
    experts = out_ref.shape[0] // CAP
    routes = hidden_ref.shape[0]
    ids = ids_ref[...]
    named = (lax.broadcasted_iota(jnp.int32, (experts, routes), 0) == ids).astype(F32)
    before = lax.broadcasted_iota(jnp.int32, (routes, routes), 0) < lax.broadcasted_iota(
        jnp.int32, (routes, routes), 1
    )
    earlier = dot(named.astype(BF16), before.astype(F32).astype(BF16), ((1,), (0,)))
    rank = jnp.sum(named * earlier, axis=0, keepdims=True)
    place = ids * CAP + rank.astype(jnp.int32)
    hidden, facts = hidden_ref[...], facts_ref[...]
    width = hidden.shape[1]
    step = 512
    for first in range(0, experts * CAP, step):
        slots = lax.broadcasted_iota(jnp.int32, (step, routes), 0) + first
        pick = (slots == place).astype(F32).astype(BF16)
        out_ref[first : first + step, :width] = dot(pick, hidden, ((1,), (0,))).astype(BF16)
        out_ref[first : first + step, width:] = dot(pick, facts, ((1,), (0,))).astype(BF16)


def place_routes(ids_row, hidden, facts, experts):
    return pl.pallas_call(
        place_kernel,
        out_shape=jax.ShapeDtypeStruct((experts * CAP, hidden.shape[1] + FACTS), BF16),
        compiler_params=params(),
    )(ids_row, hidden, facts)


def rows_kernel(order_ref, x_ref, w_ref, *refs):
    *out_refs, x_s = refs
    groups, cap, width = x_ref.shape
    for j in range(groups):
        x_s[j * cap : (j + 1) * cap, :] = x_ref[order_ref[j]]
    width_f, width_d = w_ref.shape[1:]
    each = groups // len(out_refs)
    tile = 1024
    for n in range(0, width_d, tile):
        rows = dot(x_s[:, :width_f], w_ref[0, :, n : n + tile], ((1,), (0,))).astype(BF16)
        for j, out_ref in enumerate(out_refs):
            part = rows[j * each * cap : (j + 1) * each * cap]
            out_ref[:, :, n : n + tile] = part.reshape(each, cap, tile)
    for j, out_ref in enumerate(out_refs):
        part = x_s[j * each * cap : (j + 1) * each * cap, width_f:]
        out_ref[:, :, width_d:] = part.reshape(each, cap, FACTS)


def expert_rows(order, arrived, weight, outs):
    groups, slots, width_x = arrived.shape
    local, width_f, width_d = weight.shape
    each = groups // outs
    width = width_d + FACTS
    spec = pl.BlockSpec((each, CAP, width), lambda l, order: (0, l, 0))
    return pl.pallas_call(
        rows_kernel,
        grid_spec=pltpu.PrefetchScalarGridSpec(
            num_scalar_prefetch=1,
            grid=(local,),
            in_specs=[
                pl.BlockSpec((groups, CAP, width_x), lambda l, order: (0, l, 0)),
                pl.BlockSpec((1, width_f, width_d), lambda l, order: (l, 0, 0)),
            ],
            out_specs=[spec] * outs,
            scratch_shapes=[pltpu.VMEM((groups * CAP, width_x), BF16)],
        ),
        out_shape=[jax.ShapeDtypeStruct((each, slots, width), BF16)] * outs,
        cost_estimate=pl.CostEstimate(
            flops=2 * groups * slots * width_f * width_d,
            bytes_accessed=2 * (weight.size + arrived.size + groups * slots * width),
            transcendentals=0,
        ),
        compiler_params=params(),
    )(order, arrived, weight)


def selection(facts, tokens):
    here = lax.broadcasted_iota(jnp.int32, (facts.shape[0], tokens), 1).astype(F32)
    facts = facts.astype(F32)
    mine = here == facts[:, 0:1]
    high = jnp.where(mine, facts[:, 1:2], 0.0).astype(BF16)
    low = jnp.where(mine, facts[:, 2:3], 0.0).astype(BF16)
    return high, low


def middle_kernel(*refs):
    sel_s = refs[-1]
    owners, tokens = sel_s.shape[0], sel_s.shape[2] // 2
    outs = 1 if len(refs) == 4 else owners
    count = (len(refs) - outs - 1) // 2
    row_refs, facts_refs = refs[:count], refs[count : 2 * count]
    out_refs = refs[2 * count : -1]

    def of_owner(blocks, o):
        if len(blocks) == 1:
            return blocks[0][:, o].reshape(-1, blocks[0].shape[-1])
        return jnp.concatenate([ref[o] for ref in blocks], axis=0)

    @pl.when(pl.program_id(0) == 0)
    def _():
        for o in range(owners):
            high, low = selection(of_owner(facts_refs, o), tokens)
            sel_s[o, :, :tokens] = high
            sel_s[o, :, tokens:] = low

    for o in range(owners):
        both = dot(sel_s[o], of_owner(row_refs, o), ((0,), (0,)))
        total = both[:tokens] + both[tokens:]
        if outs == 1:
            out_refs[0][o] = total.astype(out_refs[0].dtype)
        else:
            out_refs[o][...] = total.astype(out_refs[o].dtype)


def middle_sums(rows, tokens):
    owners = SIDE
    slots, width = rows[0].shape[-2:]
    width -= FACTS
    tile = 512
    if len(rows) == 1:
        sources = rows[0].shape[0]
        row_specs = [pl.BlockSpec((sources, owners, slots, tile), lambda n: (0, 0, 0, n))]
        facts_specs = [
            pl.BlockSpec((sources, owners, slots, FACTS), lambda n: (0, 0, 0, width // FACTS))
        ]
        out_specs = [pl.BlockSpec((owners, tokens, tile), lambda n: (0, 0, n))]
        out_shape = [jax.ShapeDtypeStruct((owners, tokens, width), BF16)]
    else:
        sources = len(rows)
        row_specs = [pl.BlockSpec((owners, slots, tile), lambda n: (0, 0, n))] * sources
        facts_specs = [
            pl.BlockSpec((owners, slots, FACTS), lambda n: (0, 0, width // FACTS))
        ] * sources
        out_specs = [pl.BlockSpec((tokens, tile), lambda n: (0, n))] * owners
        out_shape = [jax.ShapeDtypeStruct((tokens, width), F32)]
        out_shape += [jax.ShapeDtypeStruct((tokens, width), BF16)] * (owners - 1)
    return pl.pallas_call(
        middle_kernel,
        grid=(width // tile,),
        in_specs=row_specs + facts_specs,
        out_specs=out_specs,
        out_shape=out_shape,
        scratch_shapes=[pltpu.VMEM((owners, sources * slots, 2 * tokens), BF16)],
        cost_estimate=pl.CostEstimate(
            flops=4 * owners * sources * slots * tokens * width,
            bytes_accessed=2 * owners * sources * slots * width,
            transcendentals=0,
        ),
        compiler_params=params(),
    )(*rows, *rows)


def token_kernel(part_ref, *refs):
    primal, tangent = refs[:SIDE], refs[SIDE]
    li_ref, up_ref = refs[SIDE + 1 : SIDE + 3]
    out_refs, grad_s = refs[SIDE + 3 : -1], refs[-1]
    summed = li_ref[...].astype(F32)
    for ref in primal:
        summed += ref[...].astype(F32)
    mt = tangent[0].astype(F32)
    for i in range(1, SIDE):
        mt += tangent[i].astype(F32)
    up = up_ref[...].astype(F32)
    width = up.shape[1]
    inverse = lax.rsqrt(jnp.sum(summed * summed, axis=1, keepdims=True) / width + EPSILON)
    cube = inverse * inverse * inverse
    a = jnp.sum(up * summed, axis=1, keepdims=True) / width
    s = jnp.sum(summed * mt, axis=1, keepdims=True) / width
    u = jnp.sum(up * mt, axis=1, keepdims=True) / width
    by_summed = 3.0 * cube * inverse * inverse * s * a - cube * u
    grad = (-cube * s) * up + by_summed * summed - (cube * a) * mt
    parts = len(out_refs)
    quarter = width // parts
    for p in range(parts):
        grad_s[p] = grad[:, p * quarter : (p + 1) * quarter].astype(BF16)
    for p in range(parts):
        out_refs[p][...] = grad_s[(part_ref[0] + p) % parts]


def token_gradients(part, primal, tangent, layer_input, upstream, parts):
    tokens, width = layer_input.shape
    tile = 16
    quarter = width // parts
    spec = pl.BlockSpec((tile, width), lambda n, part: (n, 0))
    return pl.pallas_call(
        token_kernel,
        grid_spec=pltpu.PrefetchScalarGridSpec(
            num_scalar_prefetch=1,
            grid=(tokens // tile,),
            in_specs=[spec] * SIDE
            + [pl.BlockSpec((SIDE, tile, width), lambda n, part: (0, n, 0)), spec, spec],
            out_specs=[pl.BlockSpec((tile, quarter), lambda n, part: (n, 0))] * parts,
            scratch_shapes=[pltpu.VMEM((parts, tile, quarter), BF16)],
        ),
        out_shape=[jax.ShapeDtypeStruct((tokens, quarter), BF16)] * parts,
        compiler_params=params(),
    )(part, *primal, tangent, layer_input, upstream)


def turn_kernel(hidden_ref, out_ref):
    _, groups, cap, width = hidden_ref.shape
    out_ref[0, 0] = hidden_ref[0].reshape(groups * cap, width)[:, : out_ref.shape[2]].T


def turned(hidden, local):
    parts, groups, slots, width_x = hidden.shape
    width = width_x - FACTS
    return pl.pallas_call(
        turn_kernel,
        grid=(parts, local),
        in_specs=[pl.BlockSpec((1, groups, CAP, width_x), lambda g, l: (g, 0, l, 0))],
        out_specs=pl.BlockSpec((1, 1, width, groups * CAP), lambda g, l: (g, l, 0, 0)),
        out_shape=jax.ShapeDtypeStruct((parts, local, width, groups * CAP), BF16),
        cost_estimate=pl.CostEstimate(
            flops=0, bytes_accessed=4 * hidden.size, transcendentals=0
        ),
        compiler_params=params(),
    )(hidden)


def estimate_kernel(part_ref, facts_ref, hidden_ref, grad_ref, probe_ref, out_ref, rows_s):
    step = pl.program_id(0)
    groups, _, tokens, quarter = grad_ref.shape
    local = out_ref.shape[0]
    slots = local * CAP
    nothing = jnp.zeros((slots, tokens), BF16)
    for i in range(0, groups, 2):
        high0, low0 = selection(facts_ref[0, i], tokens)
        high1, low1 = selection(facts_ref[0, i + 1], tokens)
        first = jnp.concatenate([high0, nothing, low0, nothing], axis=0)
        second = jnp.concatenate([nothing, high1, nothing, low1], axis=0)
        sel = jnp.concatenate([first, second], axis=1)
        grads = grad_ref[i : i + 2, 0].reshape(2 * tokens, quarter)
        both = dot(sel, grads, ((1,), (0,)))
        rows = (both[: 2 * slots] + both[2 * slots :]).astype(BF16)
        for j in range(2):
            for l in range(local):
                start = j * slots + l * CAP
                rows_s[l, (i + j) * CAP : (i + j + 1) * CAP, :] = rows[start : start + CAP]
    for l in range(local):
        part = dot(hidden_ref[0, l], rows_s[l], ((1,), (0,)))

        @pl.when(step == 0)
        def _():
            out_ref[l] = part

        @pl.when(jnp.logical_and(step > 0, step < pl.num_programs(0) - 1))
        def _():
            out_ref[l] += part

        @pl.when(step == pl.num_programs(0) - 1)
        def _():
            out_ref[l] = (out_ref[l] + part) * probe_ref[l].astype(F32)


def estimate(part, arrived, hidden, grads, probe):
    parts, local, width_f, slots = hidden.shape
    groups, _, tokens, quarter = grads.shape

    def group(s, part):
        return (part[0] + parts - s) % parts

    return pl.pallas_call(
        estimate_kernel,
        grid_spec=pltpu.PrefetchScalarGridSpec(
            num_scalar_prefetch=1,
            grid=(parts,),
            in_specs=[
                pl.BlockSpec(
                    (1, groups, local * CAP, FACTS), lambda s, p: (group(s, p), 0, 0, width_f // FACTS)
                ),
                pl.BlockSpec((1, local, width_f, slots), lambda s, p: (group(s, p), 0, 0, 0)),
                pl.BlockSpec((groups, 1, tokens, quarter), lambda s, p: (0, s, 0, 0)),
                pl.BlockSpec((local, width_f, quarter), lambda s, p: (0, 0, p[0])),
            ],
            out_specs=pl.BlockSpec((local, width_f, quarter), lambda s, p: (0, 0, 0)),
            scratch_shapes=[pltpu.VMEM((local, slots, quarter), BF16)],
        ),
        out_shape=jax.ShapeDtypeStruct((local, width_f, quarter), F32),
        cost_estimate=pl.CostEstimate(
            flops=2 * parts * slots * local * width_f * quarter,
            bytes_accessed=2 * (hidden.size + grads.size) + 6 * local * width_f * quarter,
            transcendentals=0,
        ),
        compiler_params=params(),
    )(part, arrived, hidden, grads, probe)


def shards(layer_input, upstream, hidden, route_ids, route_prob, down_weight, probe_signs):
    tokens, top = route_ids.shape
    local, width_f, width_d = down_weight.shape
    groups, parts = lax.axis_size("expert"), lax.axis_size("dp")
    experts = local * groups
    me, part = lax.axis_index("expert"), lax.axis_index("dp")
    x, y, core = me // (SIDE * CORES), me // CORES % SIDE, me % CORES
    side, cores = jnp.arange(SIDE, dtype=jnp.int32), jnp.arange(CORES, dtype=jnp.int32)

    combine = route_prob / jnp.sum(route_prob, axis=1, keepdims=True)
    flat = combine.reshape(-1)
    high = lax.reduce_precision(flat, 8, 7)
    high, low = high.astype(BF16), (flat - high).astype(BF16)
    owner = (jnp.arange(tokens * top, dtype=jnp.int32) // top).astype(BF16)
    facts = jnp.pad(jnp.stack([owner, high, low], axis=1), ((0, 0), (0, FACTS - 3)))
    outgoing = place_routes(route_ids.reshape(1, -1), hidden.reshape(-1, width_f), facts, experts)
    arrived = lax.all_to_all(
        outgoing.reshape(groups, local * CAP, -1), "expert", 0, 0, tiled=True
    )

    order = device_at(
        side[:, None, None], side[None, None, :], cores[None, :, None]
    ).reshape(-1)
    (rows,) = expert_rows(order, arrived, probe_signs, 1)
    lines = [
        [device_at(i, j, c) for i in range(SIDE) for c in range(CORES)] for j in range(SIDE)
    ]
    tangent_rows = lax.all_to_all(
        rows.reshape(SIDE * CORES, SIDE, local * CAP, -1),
        "expert",
        0,
        0,
        axis_index_groups=lines,
        tiled=True,
    )
    order = device_at(
        (x + side)[None, None, :] % SIDE,
        (y + side)[:, None, None] % SIDE,
        (core ^ cores)[None, :, None],
    ).reshape(-1)
    rows = expert_rows(order, arrived, down_weight, SIDE * CORES)
    primal_rows = [rows[0]]
    primal_rows += [
        shift(rows[i], 0, i // CORES, i % CORES) for i in range(1, SIDE * CORES)
    ]
    tangent_rows, *primal_rows = lax.optimization_barrier((tangent_rows, *primal_rows))
    arrived_all = lax.all_gather(arrived, "dp", axis=0, tiled=False)
    hidden_all = turned(arrived_all, local)

    (sums,) = middle_sums([tangent_rows], tokens)
    columns = [[device_at(i, j, c) for j in range(SIDE)] for i in range(SIDE) for c in range(CORES)]
    tangent = lax.all_to_all(sums, "expert", 0, 0, axis_index_groups=columns, tiled=True)
    sums = middle_sums(primal_rows, tokens)
    primal = [sums[0]] + [shift(sums[i], i, 0, 0) for i in range(1, SIDE)]

    part_row = part.astype(jnp.int32).reshape(1)
    grads = token_gradients(part_row, primal, tangent, layer_input, upstream, parts)
    grads = [grads[0]] + [
        lax.ppermute(grads[i], "dp", [(j, (j + i) % parts) for j in range(parts)])
        for i in range(1, parts)
    ]
    grads_all = lax.all_gather(jnp.stack(grads), "expert", axis=0, tiled=False)

    return estimate(part_row, arrived_all, hidden_all, grads_all, probe_signs)


def solution(mesh):
    in_specs = (
        P(("dp", "expert"), None),
        P(("dp", "expert"), None),
        P(("dp", "expert"), None, None),
        P(("dp", "expert"), None),
        P(("dp", "expert"), None),
        P("expert", None, None),
        P("expert", None, None),
    )
    out_specs = P("expert", None, "dp")
    return jax.shard_map(shards, mesh=mesh, in_specs=in_specs, out_specs=out_specs, check_vma=False)
```

```python
import jax
import jax.numpy as jnp
from jax import lax
from jax.experimental import pallas as pl
from jax.experimental.pallas import tpu as pltpu
from jax.sharding import PartitionSpec as P

EPSILON = 1e-06
CAP = 16
VMEM_LIMIT = 56 * 1024 * 1024
SIDE = 4
CORES = 2
F32 = jnp.float32
BF16 = jnp.bfloat16


def params():
    return pltpu.CompilerParams(vmem_limit_bytes=VMEM_LIMIT)


def dot(a, b, dims):
    return lax.dot_general(a, b, (dims, ((), ())), preferred_element_type=F32)


def device_at(x, y, core):
    return (x * SIDE + y) * CORES + core


def shift(value, dx, dy, core):
    pairs = []
    for i in range(SIDE * SIDE * CORES):
        x, y, c = i // (SIDE * CORES), i // CORES % SIDE, i % CORES
        pairs.append((i, device_at((x + dx) % SIDE, (y + dy) % SIDE, c ^ core)))
    return lax.ppermute(value, "expert", pairs)


def place_kernel(ids_ref, hidden_ref, out_ref, place_s):
    routes = hidden_ref.shape[0]
    experts = out_ref.shape[0] * pl.num_programs(0) // CAP
    step = out_ref.shape[0]

    @pl.when(pl.program_id(0) == 0)
    def _():
        ids = ids_ref[...]
        named = (lax.broadcasted_iota(jnp.int32, (experts, routes), 0) == ids).astype(F32)
        before = lax.broadcasted_iota(jnp.int32, (routes, routes), 0) < lax.broadcasted_iota(
            jnp.int32, (routes, routes), 1
        )
        earlier = dot(named.astype(BF16), before.astype(F32).astype(BF16), ((1,), (0,)))
        rank = jnp.sum(named * earlier, axis=0, keepdims=True)
        place_s[...] = ids * CAP + rank.astype(jnp.int32)

    slots = lax.broadcasted_iota(jnp.int32, (step, routes), 0) + pl.program_id(0) * step
    pick = (slots == place_s[...]).astype(F32).astype(BF16)
    out_ref[...] = dot(pick, hidden_ref[...], ((1,), (0,))).astype(BF16)


def place_routes(ids_row, hidden, experts):
    routes, width = hidden.shape
    step = 512
    return pl.pallas_call(
        place_kernel,
        grid=(experts * CAP // step,),
        in_specs=[
            pl.BlockSpec((1, routes), lambda i: (0, 0)),
            pl.BlockSpec((routes, width), lambda i: (0, 0)),
        ],
        out_specs=pl.BlockSpec((step, width), lambda i: (i, 0)),
        out_shape=jax.ShapeDtypeStruct((experts * CAP, width), BF16),
        scratch_shapes=[pltpu.VMEM((1, routes), jnp.int32)],
        compiler_params=params(),
    )(ids_row, hidden)


def rows_kernel(order_ref, x_ref, w_ref, *refs):
    *out_refs, x_s = refs
    groups, cap, width = x_ref.shape
    for j in range(groups):
        x_s[j * cap : (j + 1) * cap, :] = x_ref[order_ref[j]]
    width_d = w_ref.shape[2]
    each = groups // len(out_refs)
    tile = 1024
    for n in range(0, width_d, tile):
        rows = dot(x_s[...], w_ref[0, :, n : n + tile], ((1,), (0,))).astype(BF16)
        for j, out_ref in enumerate(out_refs):
            part = rows[j * each * cap : (j + 1) * each * cap]
            out_ref[:, :, n : n + tile] = part.reshape(each, cap, tile)


def expert_rows(order, arrived, weight, outs):
    groups, slots, _ = arrived.shape
    local, width_f, width_d = weight.shape
    each = groups // outs
    spec = pl.BlockSpec((each, CAP, width_d), lambda l, order: (0, l, 0))
    return pl.pallas_call(
        rows_kernel,
        grid_spec=pltpu.PrefetchScalarGridSpec(
            num_scalar_prefetch=1,
            grid=(local,),
            in_specs=[
                pl.BlockSpec((groups, CAP, width_f), lambda l, order: (0, l, 0)),
                pl.BlockSpec((1, width_f, width_d), lambda l, order: (l, 0, 0)),
            ],
            out_specs=[spec] * outs,
            scratch_shapes=[pltpu.VMEM((groups * CAP, width_f), BF16)],
        ),
        out_shape=[jax.ShapeDtypeStruct((each, slots, width_d), BF16)] * outs,
        cost_estimate=pl.CostEstimate(
            flops=2 * groups * slots * width_f * width_d,
            bytes_accessed=2 * (weight.size + arrived.size + groups * slots * width_d),
            transcendentals=0,
        ),
        compiler_params=params(),
    )(order, arrived, weight)


def selection(rank, weight):
    experts, tokens = rank.shape
    slot = lax.broadcasted_iota(jnp.int32, (CAP, tokens), 0)
    parts = [
        jnp.where(rank[e : e + 1, :] == slot, weight[e : e + 1, :], 0.0) for e in range(experts)
    ]
    return jnp.concatenate(parts, axis=0)


def split_high_low(x):
    high = x.astype(BF16)
    return high, (x - high.astype(F32)).astype(BF16)


def middle_kernel(rank_ref, weight_ref, tangent_ref, *refs):
    count = SIDE * CORES
    primal_refs, tangent_out = refs[:count], refs[count]
    primal_outs, sel_s = refs[count + 1 : -1], refs[-1]
    owners, tokens, _ = tangent_out.shape

    @pl.when(pl.program_id(0) == 0)
    def _():
        for i in range(2):
            for o in range(owners):
                high, low = split_high_low(selection(rank_ref[i, o], weight_ref[i, o]).T)
                sel_s[i, o, :tokens] = high
                sel_s[i, o, tokens:] = low

    for o in range(owners):
        rows = tangent_ref[:, o].reshape(-1, tangent_ref.shape[-1])
        both = dot(sel_s[0, o], rows, ((1,), (0,)))
        tangent_out[o] = (both[:tokens] + both[tokens:]).astype(BF16)
        rows = jnp.concatenate([ref[o] for ref in primal_refs], axis=0)
        both = dot(sel_s[1, o], rows, ((1,), (0,)))
        primal_outs[o][...] = (both[:tokens] + both[tokens:]).astype(primal_outs[o].dtype)


def middle_sums(rank, weight, tangent, primal):
    _, owners, experts, tokens = rank.shape
    sources = len(primal)
    slots, width = primal[0].shape[-2:]
    tile = 512
    whole = pl.BlockSpec(rank.shape, lambda n: (0, 0, 0, 0))
    return pl.pallas_call(
        middle_kernel,
        grid=(width // tile,),
        in_specs=[whole, whole]
        + [pl.BlockSpec((sources, owners, slots, tile), lambda n: (0, 0, 0, n))]
        + [pl.BlockSpec((owners, slots, tile), lambda n: (0, 0, n))] * sources,
        out_specs=[pl.BlockSpec((owners, tokens, tile), lambda n: (0, 0, n))]
        + [pl.BlockSpec((tokens, tile), lambda n: (0, n))] * owners,
        out_shape=[jax.ShapeDtypeStruct((owners, tokens, width), BF16)]
        + [jax.ShapeDtypeStruct((tokens, width), F32)]
        + [jax.ShapeDtypeStruct((tokens, width), BF16)] * (owners - 1),
        scratch_shapes=[pltpu.VMEM((2, owners, 2 * tokens, experts * CAP), BF16)],
        cost_estimate=pl.CostEstimate(
            flops=8 * owners * sources * slots * tokens * width,
            bytes_accessed=4 * owners * sources * slots * width,
            transcendentals=0,
        ),
        compiler_params=params(),
    )(rank, weight, tangent, *primal)


def token_kernel(part_ref, *refs):
    primal, tangent = refs[:SIDE], refs[SIDE]
    li_ref, up_ref = refs[SIDE + 1 : SIDE + 3]
    out_refs, grad_s = refs[SIDE + 3 : -1], refs[-1]
    summed = li_ref[...].astype(F32)
    for ref in primal:
        summed += ref[...].astype(F32)
    mt = tangent[0].astype(F32)
    for i in range(1, SIDE):
        mt += tangent[i].astype(F32)
    up = up_ref[...].astype(F32)
    width = up.shape[1]
    inverse = lax.rsqrt(jnp.sum(summed * summed, axis=1, keepdims=True) / width + EPSILON)
    cube = inverse * inverse * inverse
    a = jnp.sum(up * summed, axis=1, keepdims=True) / width
    s = jnp.sum(summed * mt, axis=1, keepdims=True) / width
    u = jnp.sum(up * mt, axis=1, keepdims=True) / width
    by_summed = 3.0 * cube * inverse * inverse * s * a - cube * u
    grad = (-cube * s) * up + by_summed * summed - (cube * a) * mt
    parts = len(out_refs)
    quarter = width // parts
    for p in range(parts):
        grad_s[p] = grad[:, p * quarter : (p + 1) * quarter].astype(BF16)
    for p in range(parts):
        out_refs[p][...] = grad_s[(part_ref[0] + p) % parts]


def token_gradients(part, primal, tangent, layer_input, upstream, parts):
    tokens, width = layer_input.shape
    tile = 32
    quarter = width // parts
    spec = pl.BlockSpec((tile, width), lambda n, part: (n, 0))
    return pl.pallas_call(
        token_kernel,
        grid_spec=pltpu.PrefetchScalarGridSpec(
            num_scalar_prefetch=1,
            grid=(tokens // tile,),
            in_specs=[spec] * SIDE
            + [pl.BlockSpec((SIDE, tile, width), lambda n, part: (0, n, 0)), spec, spec],
            out_specs=[pl.BlockSpec((tile, quarter), lambda n, part: (n, 0))] * parts,
            scratch_shapes=[pltpu.VMEM((parts, tile, quarter), BF16)],
        ),
        out_shape=[jax.ShapeDtypeStruct((tokens, quarter), BF16)] * parts,
        compiler_params=params(),
    )(part, *primal, tangent, layer_input, upstream)


def turn_kernel(hidden_ref, out_ref):
    _, groups, cap, width = hidden_ref.shape
    out_ref[0, 0] = hidden_ref[0].reshape(groups * cap, width).T


def turned(hidden, local):
    parts, groups, slots, width = hidden.shape
    return pl.pallas_call(
        turn_kernel,
        grid=(parts, local),
        in_specs=[pl.BlockSpec((1, groups, CAP, width), lambda g, l: (g, 0, l, 0))],
        out_specs=pl.BlockSpec((1, 1, width, groups * CAP), lambda g, l: (g, l, 0, 0)),
        out_shape=jax.ShapeDtypeStruct((parts, local, width, groups * CAP), BF16),
        cost_estimate=pl.CostEstimate(
            flops=0, bytes_accessed=4 * hidden.size, transcendentals=0
        ),
        compiler_params=params(),
    )(hidden)


def estimate_kernel(
    part_ref, rank_ref, weight_ref, hidden_ref, grad_ref, probe_ref, out_ref, rows_s, total_s
):
    step = pl.program_id(0)
    groups, _, tokens, quarter = grad_ref.shape
    local = total_s.shape[0]
    steps = pl.num_programs(0) - local
    slots = local * CAP
    nothing = jnp.zeros((slots, tokens), BF16)

    @pl.when(step < steps)
    def _():
        for i in range(0, groups, 2):
            high0, low0 = split_high_low(selection(rank_ref[0, i], weight_ref[0, i]))
            high1, low1 = split_high_low(selection(rank_ref[0, i + 1], weight_ref[0, i + 1]))
            first = jnp.concatenate([high0, nothing, low0, nothing], axis=0)
            second = jnp.concatenate([nothing, high1, nothing, low1], axis=0)
            sel = jnp.concatenate([first, second], axis=1)
            grads = grad_ref[i : i + 2, 0].reshape(2 * tokens, quarter)
            both = dot(sel, grads, ((1,), (0,)))
            rows = (both[: 2 * slots] + both[2 * slots :]).astype(BF16)
            for j in range(2):
                for l in range(local):
                    start = j * slots + l * CAP
                    rows_s[l, (i + j) * CAP : (i + j + 1) * CAP, :] = rows[start : start + CAP]

    for l in range(local):

        @pl.when(step == 0)
        def _():
            total_s[l] = dot(hidden_ref[0, l], rows_s[l], ((1,), (0,)))

        @pl.when(jnp.logical_and(step > 0, step < steps))
        def _():
            total_s[l] += dot(hidden_ref[0, l], rows_s[l], ((1,), (0,)))

    @pl.when(step >= steps)
    def _():
        out_ref[0] = total_s[step - steps] * probe_ref[0].astype(F32)


def estimate(part, rank, weight, hidden, grads, probe):
    parts, local, width_f, slots = hidden.shape
    groups, _, tokens, quarter = grads.shape

    def group(s, part):
        return (part[0] + parts - jnp.minimum(s, parts - 1)) % parts

    def expert(s):
        return jnp.maximum(s - parts, 0)

    routes = pl.BlockSpec((1, groups, local, tokens), lambda s, p: (group(s, p), 0, 0, 0))
    return pl.pallas_call(
        estimate_kernel,
        grid_spec=pltpu.PrefetchScalarGridSpec(
            num_scalar_prefetch=1,
            grid=(parts + local,),
            in_specs=[
                routes,
                routes,
                pl.BlockSpec((1, local, width_f, slots), lambda s, p: (group(s, p), 0, 0, 0)),
                pl.BlockSpec(
                    (groups, 1, tokens, quarter), lambda s, p: (0, jnp.minimum(s, parts - 1), 0, 0)
                ),
                pl.BlockSpec((1, width_f, quarter), lambda s, p: (expert(s), 0, p[0])),
            ],
            out_specs=pl.BlockSpec((1, width_f, quarter), lambda s, p: (expert(s), 0, 0)),
            scratch_shapes=[
                pltpu.VMEM((local, slots, quarter), BF16),
                pltpu.VMEM((local, width_f, quarter), F32),
            ],
        ),
        out_shape=jax.ShapeDtypeStruct((local, width_f, quarter), F32),
        cost_estimate=pl.CostEstimate(
            flops=2 * parts * slots * local * width_f * quarter,
            bytes_accessed=2 * (hidden.size + grads.size) + 6 * local * width_f * quarter,
            transcendentals=0,
        ),
        compiler_params=params(),
    )(part, rank, weight, hidden, grads, probe)


def routes_to(experts, ids, weights):
    tokens = ids.shape[-1]
    match = ids[:, None, :, :] == experts[..., :, None, None]
    named = jnp.any(match, axis=2)
    weight = jnp.sum(jnp.where(match, weights[:, None, :, :], 0.0), axis=2)
    before = jnp.triu(jnp.ones((tokens, tokens), F32), 1).astype(BF16)
    earlier = jnp.einsum("blt,tu->blu", named.astype(BF16), before, preferred_element_type=F32)
    return jnp.where(named, earlier.astype(jnp.int32), -1), weight


def shards(layer_input, upstream, hidden, route_ids, route_prob, down_weight, probe_signs):
    tokens, top = route_ids.shape
    local, width_f, width_d = down_weight.shape
    groups, parts = lax.axis_size("expert"), lax.axis_size("dp")
    experts = local * groups
    me, part = lax.axis_index("expert"), lax.axis_index("dp")
    x, y, core = me // (SIDE * CORES), me // CORES % SIDE, me % CORES
    side, cores = jnp.arange(SIDE, dtype=jnp.int32), jnp.arange(CORES, dtype=jnp.int32)

    combine = route_prob / jnp.sum(route_prob, axis=1, keepdims=True)
    facts = jnp.concatenate([route_ids.T.astype(F32), combine.T], axis=0)
    lines = [facts] + [shift(facts, 0, i, 0) for i in range(1, SIDE)]
    lines += [facts] + [shift(facts, i, 0, 0) for i in range(1, SIDE)]
    outgoing = place_routes(route_ids.reshape(1, -1), hidden.reshape(-1, width_f), experts)
    arrived = lax.all_to_all(
        outgoing.reshape(groups, local * CAP, -1), "expert", 0, 0, tiled=True
    )

    arrived, *lines[:-1] = lax.optimization_barrier((arrived, *lines[:-1]))

    order = device_at(
        side[:, None, None], side[None, None, :], cores[None, :, None]
    ).reshape(-1)
    (rows,) = expert_rows(order, arrived, probe_signs, 1)
    rows, lines[-1] = lax.optimization_barrier((rows, lines[-1]))
    along_x = [
        [device_at(i, j, c) for i in range(SIDE) for c in range(CORES)] for j in range(SIDE)
    ]
    tangent_rows = lax.all_to_all(
        rows.reshape(SIDE * CORES, SIDE, local * CAP, -1),
        "expert",
        0,
        0,
        axis_index_groups=along_x,
        tiled=True,
    )
    order = device_at(
        (x + side)[None, None, :] % SIDE,
        (y + side)[:, None, None] % SIDE,
        (core ^ cores)[None, :, None],
    ).reshape(-1)
    rows = expert_rows(order, arrived, down_weight, SIDE * CORES)
    primal_rows = [rows[0]]
    primal_rows += [
        shift(rows[i], 0, i // CORES, i % CORES) for i in range(1, SIDE * CORES)
    ]
    arrived_all = lax.all_gather(arrived, "dp", axis=0, tiled=False)
    hidden_all = turned(arrived_all, local)

    steps = jnp.concatenate([(y - side) % SIDE, SIDE + -side % SIDE])
    chosen = jnp.take(jnp.stack(lines), steps, axis=0)
    devices = jnp.stack(
        [
            device_at(side[:, None], y, cores[None, :]).reshape(-1),
            device_at(x, (y - side[:, None]) % SIDE, core ^ cores[None, :]).reshape(-1),
        ]
    )
    listed = (devices[:, :, None] * local + jnp.arange(local, dtype=jnp.int32)).reshape(2, -1)
    rank, weight = routes_to(
        jnp.repeat(listed, SIDE, axis=0), chosen[:, :top].astype(jnp.int32), chosen[:, top:]
    )
    rank, weight = (a.reshape(2, SIDE, -1, tokens) for a in (rank, weight))

    tangent_rows, *primal_rows = lax.optimization_barrier((tangent_rows, *primal_rows))
    sums, *primal = middle_sums(rank, weight, tangent_rows, primal_rows)
    along_y = [[device_at(i, j, c) for j in range(SIDE)] for i in range(SIDE) for c in range(CORES)]
    tangent = lax.all_to_all(sums, "expert", 0, 0, axis_index_groups=along_y, tiled=True)
    primal = [primal[0]] + [shift(primal[i], i, 0, 0) for i in range(1, SIDE)]
    tangent, hidden_all = lax.optimization_barrier((tangent, hidden_all))

    part_row = part.astype(jnp.int32).reshape(1)
    grads = token_gradients(part_row, primal, tangent, layer_input, upstream, parts)
    grads = [grads[0]] + [
        lax.ppermute(grads[i], "dp", [(j, (j + i) % parts) for j in range(parts)])
        for i in range(1, parts)
    ]
    ids, weights, grads = lax.optimization_barrier((route_ids.T, combine.T, jnp.stack(grads)))
    grads_all = lax.all_gather(grads, "expert", axis=0, tiled=False)
    ids = lax.all_gather(ids, ("dp", "expert"), axis=0, tiled=False)
    weights = lax.all_gather(weights, ("dp", "expert"), axis=0, tiled=False)
    own = me * local + jnp.arange(local, dtype=jnp.int32)
    rank, weight = routes_to(own, ids, weights)
    rank = rank.reshape(parts, groups, local, tokens)
    weight = weight.reshape(parts, groups, local, tokens)
    return estimate(part_row, rank, weight, hidden_all, grads_all, probe_signs)


def solution(mesh):
    in_specs = (
        P(("dp", "expert"), None),
        P(("dp", "expert"), None),
        P(("dp", "expert"), None, None),
        P(("dp", "expert"), None),
        P(("dp", "expert"), None),
        P("expert", None, None),
        P("expert", None, None),
    )
    out_specs = P("expert", None, "dp")
    return jax.shard_map(shards, mesh=mesh, in_specs=in_specs, out_specs=out_specs, check_vma=False)
```

```python
import jax
import jax.numpy as jnp
from jax import lax
from jax.experimental import pallas as pl
from jax.experimental.pallas import tpu as pltpu
from jax.sharding import PartitionSpec as P

EPSILON = 1e-06
CAP = 16
VMEM_LIMIT = 56 * 1024 * 1024
SIDE = 4
CORES = 2
F32 = jnp.float32
BF16 = jnp.bfloat16


def params():
    return pltpu.CompilerParams(vmem_limit_bytes=VMEM_LIMIT)


def dot(a, b, dims):
    return lax.dot_general(a, b, (dims, ((), ())), preferred_element_type=F32)


def device_at(x, y, core):
    return (x * SIDE + y) * CORES + core


def shift(value, dx, dy, core):
    pairs = []
    for i in range(SIDE * SIDE * CORES):
        x, y, c = i // (SIDE * CORES), i // CORES % SIDE, i % CORES
        pairs.append((i, device_at((x + dx) % SIDE, (y + dy) % SIDE, c ^ core)))
    return lax.ppermute(value, "expert", pairs)


def place_kernel(ids_ref, hidden_ref, out_ref, place_s):
    routes = hidden_ref.shape[0]
    experts = out_ref.shape[0] * pl.num_programs(0) // CAP
    step = out_ref.shape[0]

    @pl.when(pl.program_id(0) == 0)
    def _():
        ids = ids_ref[...]
        named = (lax.broadcasted_iota(jnp.int32, (experts, routes), 0) == ids).astype(F32)
        before = lax.broadcasted_iota(jnp.int32, (routes, routes), 0) < lax.broadcasted_iota(
            jnp.int32, (routes, routes), 1
        )
        earlier = dot(named.astype(BF16), before.astype(F32).astype(BF16), ((1,), (0,)))
        rank = jnp.sum(named * earlier, axis=0, keepdims=True)
        place_s[...] = ids * CAP + rank.astype(jnp.int32)

    slots = lax.broadcasted_iota(jnp.int32, (step, routes), 0) + pl.program_id(0) * step
    pick = (slots == place_s[...]).astype(F32).astype(BF16)
    out_ref[...] = dot(pick, hidden_ref[...], ((1,), (0,))).astype(BF16)


def place_routes(ids_row, hidden, experts):
    routes, width = hidden.shape
    step = 512
    return pl.pallas_call(
        place_kernel,
        grid=(experts * CAP // step,),
        in_specs=[
            pl.BlockSpec((1, routes), lambda i: (0, 0)),
            pl.BlockSpec((routes, width), lambda i: (0, 0)),
        ],
        out_specs=pl.BlockSpec((step, width), lambda i: (i, 0)),
        out_shape=jax.ShapeDtypeStruct((experts * CAP, width), BF16),
        scratch_shapes=[pltpu.VMEM((1, routes), jnp.int32)],
        compiler_params=params(),
    )(ids_row, hidden)


def rows_kernel(order_ref, x_ref, w_ref, *refs):
    *out_refs, x_s = refs
    groups, cap, width = x_ref.shape
    for j in range(groups):
        x_s[j * cap : (j + 1) * cap, :] = x_ref[order_ref[j]]
    width_d = w_ref.shape[2]
    each = groups // len(out_refs)
    tile = 1024
    for n in range(0, width_d, tile):
        rows = dot(x_s[...], w_ref[0, :, n : n + tile], ((1,), (0,))).astype(BF16)
        for j, out_ref in enumerate(out_refs):
            part = rows[j * each * cap : (j + 1) * each * cap]
            out_ref[:, :, n : n + tile] = part.reshape(each, cap, tile)


def expert_rows(order, arrived, weight, outs):
    groups, slots, _ = arrived.shape
    local, width_f, width_d = weight.shape
    each = groups // outs
    spec = pl.BlockSpec((each, CAP, width_d), lambda l, order: (0, l, 0))
    return pl.pallas_call(
        rows_kernel,
        grid_spec=pltpu.PrefetchScalarGridSpec(
            num_scalar_prefetch=1,
            grid=(local,),
            in_specs=[
                pl.BlockSpec((groups, CAP, width_f), lambda l, order: (0, l, 0)),
                pl.BlockSpec((1, width_f, width_d), lambda l, order: (l, 0, 0)),
            ],
            out_specs=[spec] * outs,
            scratch_shapes=[pltpu.VMEM((groups * CAP, width_f), BF16)],
        ),
        out_shape=[jax.ShapeDtypeStruct((each, slots, width_d), BF16)] * outs,
        cost_estimate=pl.CostEstimate(
            flops=2 * groups * slots * width_f * width_d,
            bytes_accessed=2 * (weight.size + arrived.size + groups * slots * width_d),
            transcendentals=0,
        ),
        compiler_params=params(),
    )(order, arrived, weight)


def selection(rank, weight):
    experts, tokens = rank.shape
    slot = lax.broadcasted_iota(jnp.int32, (CAP, tokens), 0)
    parts = [
        jnp.where(rank[e : e + 1, :] == slot, weight[e : e + 1, :], 0.0) for e in range(experts)
    ]
    return jnp.concatenate(parts, axis=0)


def split_high_low(x):
    high = x.astype(BF16)
    return high, (x - high.astype(F32)).astype(BF16)


def middle_kernel(rank_ref, weight_ref, tangent_ref, *refs):
    count = SIDE * CORES
    primal_refs, tangent_out = refs[:count], refs[count]
    primal_outs, sel_s = refs[count + 1 : -1], refs[-1]
    owners, tokens, _ = tangent_out.shape

    @pl.when(pl.program_id(0) == 0)
    def _():
        for i in range(2):
            for o in range(owners):
                high, low = split_high_low(selection(rank_ref[i, o], weight_ref[i, o]).T)
                sel_s[i, o, :tokens] = high
                sel_s[i, o, tokens:] = low

    for o in range(owners):
        rows = tangent_ref[:, o].reshape(-1, tangent_ref.shape[-1])
        both = dot(sel_s[0, o], rows, ((1,), (0,)))
        tangent_out[o] = (both[:tokens] + both[tokens:]).astype(BF16)
        rows = jnp.concatenate([ref[o] for ref in primal_refs], axis=0)
        both = dot(sel_s[1, o], rows, ((1,), (0,)))
        primal_outs[o][...] = (both[:tokens] + both[tokens:]).astype(primal_outs[o].dtype)


def middle_sums(rank, weight, tangent, primal):
    _, owners, experts, tokens = rank.shape
    sources = len(primal)
    slots, width = primal[0].shape[-2:]
    tile = 512
    whole = pl.BlockSpec(rank.shape, lambda n: (0, 0, 0, 0))
    return pl.pallas_call(
        middle_kernel,
        grid=(width // tile,),
        in_specs=[whole, whole]
        + [pl.BlockSpec((sources, owners, slots, tile), lambda n: (0, 0, 0, n))]
        + [pl.BlockSpec((owners, slots, tile), lambda n: (0, 0, n))] * sources,
        out_specs=[pl.BlockSpec((owners, tokens, tile), lambda n: (0, 0, n))]
        + [pl.BlockSpec((tokens, tile), lambda n: (0, n))] * owners,
        out_shape=[jax.ShapeDtypeStruct((owners, tokens, width), BF16)]
        + [jax.ShapeDtypeStruct((tokens, width), F32)]
        + [jax.ShapeDtypeStruct((tokens, width), BF16)] * (owners - 1),
        scratch_shapes=[pltpu.VMEM((2, owners, 2 * tokens, experts * CAP), BF16)],
        cost_estimate=pl.CostEstimate(
            flops=8 * owners * sources * slots * tokens * width,
            bytes_accessed=4 * owners * sources * slots * width,
            transcendentals=0,
        ),
        compiler_params=params(),
    )(rank, weight, tangent, *primal)


def token_kernel(part_ref, *refs):
    primal, tangent = refs[:SIDE], refs[SIDE]
    li_ref, up_ref = refs[SIDE + 1 : SIDE + 3]
    out_refs, grad_s = refs[SIDE + 3 : -1], refs[-1]
    summed = li_ref[...].astype(F32)
    for ref in primal:
        summed += ref[...].astype(F32)
    mt = tangent[0].astype(F32)
    for i in range(1, SIDE):
        mt += tangent[i].astype(F32)
    up = up_ref[...].astype(F32)
    width = up.shape[1]
    inverse = lax.rsqrt(jnp.sum(summed * summed, axis=1, keepdims=True) / width + EPSILON)
    cube = inverse * inverse * inverse
    a = jnp.sum(up * summed, axis=1, keepdims=True) / width
    s = jnp.sum(summed * mt, axis=1, keepdims=True) / width
    u = jnp.sum(up * mt, axis=1, keepdims=True) / width
    by_summed = 3.0 * cube * inverse * inverse * s * a - cube * u
    grad = (-cube * s) * up + by_summed * summed - (cube * a) * mt
    parts = len(out_refs)
    quarter = width // parts
    for p in range(parts):
        grad_s[p] = grad[:, p * quarter : (p + 1) * quarter].astype(BF16)
    for p in range(parts):
        out_refs[p][...] = grad_s[(part_ref[0] + p) % parts]


def token_gradients(part, primal, tangent, layer_input, upstream, parts):
    tokens, width = layer_input.shape
    tile = 32
    quarter = width // parts
    spec = pl.BlockSpec((tile, width), lambda n, part: (n, 0))
    return pl.pallas_call(
        token_kernel,
        grid_spec=pltpu.PrefetchScalarGridSpec(
            num_scalar_prefetch=1,
            grid=(tokens // tile,),
            in_specs=[spec] * SIDE
            + [pl.BlockSpec((SIDE, tile, width), lambda n, part: (0, n, 0)), spec, spec],
            out_specs=[pl.BlockSpec((tile, quarter), lambda n, part: (n, 0))] * parts,
            scratch_shapes=[pltpu.VMEM((parts, tile, quarter), BF16)],
        ),
        out_shape=[jax.ShapeDtypeStruct((tokens, quarter), BF16)] * parts,
        compiler_params=params(),
    )(part, *primal, tangent, layer_input, upstream)


def turn_kernel(hidden_ref, out_ref):
    _, groups, cap, width = hidden_ref.shape
    out_ref[0, 0] = hidden_ref[0].reshape(groups * cap, width).T


def turned(hidden, local):
    parts, groups, slots, width = hidden.shape
    return pl.pallas_call(
        turn_kernel,
        grid=(parts, local),
        in_specs=[pl.BlockSpec((1, groups, CAP, width), lambda g, l: (g, 0, l, 0))],
        out_specs=pl.BlockSpec((1, 1, width, groups * CAP), lambda g, l: (g, l, 0, 0)),
        out_shape=jax.ShapeDtypeStruct((parts, local, width, groups * CAP), BF16),
        cost_estimate=pl.CostEstimate(
            flops=0, bytes_accessed=4 * hidden.size, transcendentals=0
        ),
        compiler_params=params(),
    )(hidden)


def estimate_kernel(
    part_ref, rank_ref, weight_ref, hidden_ref, grad_ref, probe_ref, out_ref, rows_s, total_s
):
    step = pl.program_id(0)
    groups, _, tokens, quarter = grad_ref.shape
    local = total_s.shape[0]
    steps = pl.num_programs(0) - local
    slots = local * CAP
    nothing = jnp.zeros((slots, tokens), BF16)

    @pl.when(step == 0)
    def _():
        total_s[...] = jnp.zeros(total_s.shape, F32)

    @pl.when(step < steps)
    def _():
        for i in range(0, groups, 2):
            high0, low0 = split_high_low(selection(rank_ref[0, i], weight_ref[0, i]))
            high1, low1 = split_high_low(selection(rank_ref[0, i + 1], weight_ref[0, i + 1]))
            first = jnp.concatenate([high0, nothing, low0, nothing], axis=0)
            second = jnp.concatenate([nothing, high1, nothing, low1], axis=0)
            sel = jnp.concatenate([first, second], axis=1)
            grads = grad_ref[i : i + 2, 0].reshape(2 * tokens, quarter)
            both = dot(sel, grads, ((1,), (0,)))
            rows = (both[: 2 * slots] + both[2 * slots :]).astype(BF16)
            for j in range(2):
                for l in range(local):
                    start = j * slots + l * CAP
                    rows_s[l, (i + j) * CAP : (i + j + 1) * CAP, :] = rows[start : start + CAP]

        for l in range(local):
            total_s[l] += dot(hidden_ref[0, l], rows_s[l], ((1,), (0,)))

    @pl.when(step >= steps)
    def _():
        out_ref[0] = total_s[step - steps] * probe_ref[0].astype(F32)


def estimate(part, rank, weight, hidden, grads, probe):
    parts, local, width_f, slots = hidden.shape
    groups, _, tokens, quarter = grads.shape

    def group(s, part):
        return (part[0] + parts - jnp.minimum(s, parts - 1)) % parts

    def expert(s):
        return jnp.maximum(s - parts, 0)

    routes = pl.BlockSpec((1, groups, local, tokens), lambda s, p: (group(s, p), 0, 0, 0))
    return pl.pallas_call(
        estimate_kernel,
        grid_spec=pltpu.PrefetchScalarGridSpec(
            num_scalar_prefetch=1,
            grid=(parts + local,),
            in_specs=[
                routes,
                routes,
                pl.BlockSpec((1, local, width_f, slots), lambda s, p: (group(s, p), 0, 0, 0)),
                pl.BlockSpec(
                    (groups, 1, tokens, quarter), lambda s, p: (0, jnp.minimum(s, parts - 1), 0, 0)
                ),
                pl.BlockSpec((1, width_f, quarter), lambda s, p: (expert(s), 0, p[0])),
            ],
            out_specs=pl.BlockSpec((1, width_f, quarter), lambda s, p: (expert(s), 0, 0)),
            scratch_shapes=[
                pltpu.VMEM((local, slots, quarter), BF16),
                pltpu.VMEM((local, width_f, quarter), F32),
            ],
        ),
        out_shape=jax.ShapeDtypeStruct((local, width_f, quarter), F32),
        cost_estimate=pl.CostEstimate(
            flops=2 * parts * slots * local * width_f * quarter,
            bytes_accessed=2 * (hidden.size + grads.size) + 6 * local * width_f * quarter,
            transcendentals=0,
        ),
        compiler_params=params(),
    )(part, rank, weight, hidden, grads, probe)


def routes_to(experts, ids, weights):
    tokens = ids.shape[-1]
    match = ids[:, None, :, :] == experts[..., :, None, None]
    named = jnp.any(match, axis=2)
    weight = jnp.sum(jnp.where(match, weights[:, None, :, :], 0.0), axis=2)
    before = jnp.triu(jnp.ones((tokens, tokens), F32), 1).astype(BF16)
    earlier = jnp.einsum("blt,tu->blu", named.astype(BF16), before, preferred_element_type=F32)
    return jnp.where(named, earlier.astype(jnp.int32), -1), weight


def shards(layer_input, upstream, hidden, route_ids, route_prob, down_weight, probe_signs):
    tokens, top = route_ids.shape
    local, width_f, width_d = down_weight.shape
    groups, parts = lax.axis_size("expert"), lax.axis_size("dp")
    experts = local * groups
    me, part = lax.axis_index("expert"), lax.axis_index("dp")
    x, y, core = me // (SIDE * CORES), me // CORES % SIDE, me % CORES
    side, cores = jnp.arange(SIDE, dtype=jnp.int32), jnp.arange(CORES, dtype=jnp.int32)

    combine = route_prob / jnp.sum(route_prob, axis=1, keepdims=True)
    facts = jnp.concatenate([route_ids.T.astype(F32), combine.T], axis=0)
    lines = [facts] + [shift(facts, 0, i, 0) for i in range(1, SIDE)]
    lines += [facts] + [shift(facts, i, 0, 0) for i in range(1, SIDE)]
    outgoing = place_routes(route_ids.reshape(1, -1), hidden.reshape(-1, width_f), experts)
    arrived = lax.all_to_all(
        outgoing.reshape(groups, local * CAP, -1), "expert", 0, 0, tiled=True
    )

    arrived, *lines[:-1] = lax.optimization_barrier((arrived, *lines[:-1]))

    order = device_at(
        side[:, None, None], side[None, None, :], cores[None, :, None]
    ).reshape(-1)
    (rows,) = expert_rows(order, arrived, probe_signs, 1)
    rows, lines[-1] = lax.optimization_barrier((rows, lines[-1]))
    along_x = [
        [device_at(i, j, c) for i in range(SIDE) for c in range(CORES)] for j in range(SIDE)
    ]
    tangent_rows = lax.all_to_all(
        rows.reshape(SIDE * CORES, SIDE, local * CAP, -1),
        "expert",
        0,
        0,
        axis_index_groups=along_x,
        tiled=True,
    )
    order = device_at(
        (x + side)[None, None, :] % SIDE,
        (y + side)[:, None, None] % SIDE,
        (core ^ cores)[None, :, None],
    ).reshape(-1)
    rows = expert_rows(order, arrived, down_weight, SIDE * CORES)
    primal_rows = [rows[0]]
    primal_rows += [
        shift(rows[i], 0, i // CORES, i % CORES) for i in range(1, SIDE * CORES)
    ]
    arrived_all = lax.all_gather(arrived, "dp", axis=0, tiled=False)
    hidden_all = turned(arrived_all, local)

    steps = jnp.concatenate([(y - side) % SIDE, SIDE + -side % SIDE])
    chosen = jnp.take(jnp.stack(lines), steps, axis=0)
    devices = jnp.stack(
        [
            device_at(side[:, None], y, cores[None, :]).reshape(-1),
            device_at(x, (y - side[:, None]) % SIDE, core ^ cores[None, :]).reshape(-1),
        ]
    )
    listed = (devices[:, :, None] * local + jnp.arange(local, dtype=jnp.int32)).reshape(2, -1)
    rank, weight = routes_to(
        jnp.repeat(listed, SIDE, axis=0), chosen[:, :top].astype(jnp.int32), chosen[:, top:]
    )
    rank, weight = (a.reshape(2, SIDE, -1, tokens) for a in (rank, weight))

    tangent_rows, *primal_rows = lax.optimization_barrier((tangent_rows, *primal_rows))
    sums, *primal = middle_sums(rank, weight, tangent_rows, primal_rows)
    along_y = [[device_at(i, j, c) for j in range(SIDE)] for i in range(SIDE) for c in range(CORES)]
    tangent = lax.all_to_all(sums, "expert", 0, 0, axis_index_groups=along_y, tiled=True)
    primal = [primal[0]] + [shift(primal[i], i, 0, 0) for i in range(1, SIDE)]
    tangent, hidden_all = lax.optimization_barrier((tangent, hidden_all))

    part_row = part.astype(jnp.int32).reshape(1)
    grads = token_gradients(part_row, primal, tangent, layer_input, upstream, parts)
    grads = [grads[0]] + [
        lax.ppermute(grads[i], "dp", [(j, (j + i) % parts) for j in range(parts)])
        for i in range(1, parts)
    ]
    high = lax.reduce_precision(combine, 8, 7)
    routes = jnp.concatenate([route_ids.astype(F32), high, combine - high], axis=1).T.astype(BF16)
    routes, grads = lax.optimization_barrier((routes, jnp.stack(grads)))
    grads_all = lax.all_gather(grads, "expert", axis=0, tiled=False)
    routes = lax.all_gather(routes, ("dp", "expert"), axis=0, tiled=False)
    ids = routes[:, :top].astype(jnp.int32)
    weights = routes[:, top : 2 * top].astype(F32) + routes[:, 2 * top :].astype(F32)
    own = me * local + jnp.arange(local, dtype=jnp.int32)
    rank, weight = routes_to(own, ids, weights)
    rank = rank.reshape(parts, groups, local, tokens)
    weight = weight.reshape(parts, groups, local, tokens)
    return estimate(part_row, rank, weight, hidden_all, grads_all, probe_signs)


def solution(mesh):
    in_specs = (
        P(("dp", "expert"), None),
        P(("dp", "expert"), None),
        P(("dp", "expert"), None, None),
        P(("dp", "expert"), None),
        P(("dp", "expert"), None),
        P("expert", None, None),
        P("expert", None, None),
    )
    out_specs = P("expert", None, "dp")
    return jax.shard_map(shards, mesh=mesh, in_specs=in_specs, out_specs=out_specs, check_vma=False)
```

```python
import jax
import jax.numpy as jnp
from jax import lax
from jax.experimental import pallas as pl
from jax.experimental.pallas import tpu as pltpu
from jax.sharding import PartitionSpec as P

EPSILON = 1e-06
CAP = 16
VMEM_LIMIT = 62 * 1024 * 1024
SIDE = 4
CORES = 2
LANES = 128
F32 = jnp.float32
BF16 = jnp.bfloat16


def params():
    return pltpu.CompilerParams(vmem_limit_bytes=VMEM_LIMIT)


def dot(a, b, dims):
    return lax.dot_general(a, b, (dims, ((), ())), preferred_element_type=F32)


def device_at(x, y, core):
    return (x * SIDE + y) * CORES + core


def shift(value, dx, dy, core):
    pairs = []
    for i in range(SIDE * SIDE * CORES):
        x, y, c = i // (SIDE * CORES), i // CORES % SIDE, i % CORES
        pairs.append((i, device_at((x + dx) % SIDE, (y + dy) % SIDE, c ^ core)))
    return lax.ppermute(value, "expert", pairs)


def place_kernel(ids_ref, hidden_ref, out_ref, place_s):
    routes = hidden_ref.shape[0]
    experts = out_ref.shape[0] * pl.num_programs(0) // CAP
    step = out_ref.shape[0]

    @pl.when(pl.program_id(0) == 0)
    def _():
        ids = ids_ref[...]
        named = (lax.broadcasted_iota(jnp.int32, (experts, routes), 0) == ids).astype(F32)
        token = lax.broadcasted_iota(jnp.int32, (LANES, routes), 0)
        owner = lax.broadcasted_iota(jnp.int32, (LANES, routes), 1) // (routes // LANES)
        own = (token == owner).astype(F32).astype(BF16)
        after = (token < owner).astype(F32).astype(BF16)
        by_token = dot(named.astype(BF16), own, ((1,), (1,))).astype(BF16)
        earlier = dot(by_token, after, ((1,), (0,)))
        rank = jnp.sum(named * earlier, axis=0, keepdims=True)
        place_s[...] = ids * CAP + rank.astype(jnp.int32)

    slots = lax.broadcasted_iota(jnp.int32, (step, routes), 0) + pl.program_id(0) * step
    pick = (slots == place_s[...]).astype(F32).astype(BF16)
    out_ref[...] = dot(pick, hidden_ref[...], ((1,), (0,))).astype(BF16)


def place_routes(ids_row, hidden, experts):
    routes, width = hidden.shape
    step = 512
    return pl.pallas_call(
        place_kernel,
        grid=(experts * CAP // step,),
        in_specs=[
            pl.BlockSpec((1, routes), lambda i: (0, 0)),
            pl.BlockSpec((routes, width), lambda i: (0, 0)),
        ],
        out_specs=pl.BlockSpec((step, width), lambda i: (i, 0)),
        out_shape=jax.ShapeDtypeStruct((experts * CAP, width), BF16),
        scratch_shapes=[pltpu.VMEM((1, routes), jnp.int32)],
        compiler_params=params(),
    )(ids_row, hidden)


def rows_kernel(order_ref, x_ref, w_ref, *refs):
    *out_refs, x_s = refs
    groups, cap, width = x_ref.shape
    for j in range(groups):
        x_s[j * cap : (j + 1) * cap, :] = x_ref[order_ref[j]]
    width_d = w_ref.shape[2]
    each = groups // len(out_refs)
    tile = 1024
    for n in range(0, width_d, tile):
        rows = dot(x_s[...], w_ref[0, :, n : n + tile], ((1,), (0,))).astype(BF16)
        for j, out_ref in enumerate(out_refs):
            part = rows[j * each * cap : (j + 1) * each * cap]
            out_ref[:, :, n : n + tile] = part.reshape(each, cap, tile)


def expert_rows(order, arrived, weight, outs):
    groups, slots, _ = arrived.shape
    local, width_f, width_d = weight.shape
    each = groups // outs
    spec = pl.BlockSpec((each, CAP, width_d), lambda l, order: (0, l, 0))
    return pl.pallas_call(
        rows_kernel,
        grid_spec=pltpu.PrefetchScalarGridSpec(
            num_scalar_prefetch=1,
            grid=(local,),
            in_specs=[
                pl.BlockSpec((groups, CAP, width_f), lambda l, order: (0, l, 0)),
                pl.BlockSpec((1, width_f, width_d), lambda l, order: (l, 0, 0)),
            ],
            out_specs=[spec] * outs,
            scratch_shapes=[pltpu.VMEM((groups * CAP, width_f), BF16)],
        ),
        out_shape=[jax.ShapeDtypeStruct((each, slots, width_d), BF16)] * outs,
        cost_estimate=pl.CostEstimate(
            flops=2 * groups * slots * width_f * width_d,
            bytes_accessed=2 * (weight.size + arrived.size + groups * slots * width_d),
            transcendentals=0,
        ),
        compiler_params=params(),
    )(order, arrived, weight)


def selection(rank, weight):
    experts, tokens = rank.shape
    slot = lax.broadcasted_iota(jnp.int32, (CAP, tokens), 0)
    parts = [
        jnp.where(rank[e : e + 1, :] == slot, weight[e : e + 1, :], 0.0) for e in range(experts)
    ]
    return jnp.concatenate(parts, axis=0)


def split_high_low(x):
    high = x.astype(BF16)
    return high, (x - high.astype(F32)).astype(BF16)


def middle_kernel(rank_ref, weight_ref, tangent_ref, *refs):
    count = SIDE * CORES
    primal_refs, tangent_out = refs[:count], refs[count]
    primal_outs, sel_s = refs[count + 1 : -1], refs[-1]
    owners, tokens, _ = tangent_out.shape

    @pl.when(pl.program_id(0) == 0)
    def _():
        for i in range(2):
            for o in range(owners):
                high, low = split_high_low(selection(rank_ref[i, o], weight_ref[i, o]).T)
                sel_s[i, o, :tokens] = high
                sel_s[i, o, tokens:] = low

    for o in range(owners):
        rows = tangent_ref[:, o].reshape(-1, tangent_ref.shape[-1])
        both = dot(sel_s[0, o], rows, ((1,), (0,)))
        tangent_out[o] = (both[:tokens] + both[tokens:]).astype(BF16)
        rows = jnp.concatenate([ref[o] for ref in primal_refs], axis=0)
        both = dot(sel_s[1, o], rows, ((1,), (0,)))
        primal_outs[o][...] = (both[:tokens] + both[tokens:]).astype(primal_outs[o].dtype)


def middle_sums(rank, weight, tangent, primal):
    _, owners, experts, tokens = rank.shape
    sources = len(primal)
    slots, width = primal[0].shape[-2:]
    tile = 512
    whole = pl.BlockSpec(rank.shape, lambda n: (0, 0, 0, 0))
    return pl.pallas_call(
        middle_kernel,
        grid=(width // tile,),
        in_specs=[whole, whole]
        + [pl.BlockSpec((sources, owners, slots, tile), lambda n: (0, 0, 0, n))]
        + [pl.BlockSpec((owners, slots, tile), lambda n: (0, 0, n))] * sources,
        out_specs=[pl.BlockSpec((owners, tokens, tile), lambda n: (0, 0, n))]
        + [pl.BlockSpec((tokens, tile), lambda n: (0, n))] * owners,
        out_shape=[jax.ShapeDtypeStruct((owners, tokens, width), BF16)]
        + [jax.ShapeDtypeStruct((tokens, width), F32)]
        + [jax.ShapeDtypeStruct((tokens, width), BF16)] * (owners - 1),
        scratch_shapes=[pltpu.VMEM((2, owners, 2 * tokens, experts * CAP), BF16)],
        cost_estimate=pl.CostEstimate(
            flops=8 * owners * sources * slots * tokens * width,
            bytes_accessed=4 * owners * sources * slots * width,
            transcendentals=0,
        ),
        compiler_params=params(),
    )(rank, weight, tangent, *primal)


def token_kernel(part_ref, *refs):
    primal, tangent = refs[:SIDE], refs[SIDE]
    li_ref, up_ref = refs[SIDE + 1 : SIDE + 3]
    out_refs, grad_s = refs[SIDE + 3 : -1], refs[-1]
    summed = li_ref[...].astype(F32)
    for ref in primal:
        summed += ref[...].astype(F32)
    mt = tangent[0].astype(F32)
    for i in range(1, SIDE):
        mt += tangent[i].astype(F32)
    up = up_ref[...].astype(F32)
    width = up.shape[1]
    inverse = lax.rsqrt(jnp.sum(summed * summed, axis=1, keepdims=True) / width + EPSILON)
    cube = inverse * inverse * inverse
    a = jnp.sum(up * summed, axis=1, keepdims=True) / width
    s = jnp.sum(summed * mt, axis=1, keepdims=True) / width
    u = jnp.sum(up * mt, axis=1, keepdims=True) / width
    by_summed = 3.0 * cube * inverse * inverse * s * a - cube * u
    grad = (-cube * s) * up + by_summed * summed - (cube * a) * mt
    parts = len(out_refs)
    quarter = width // parts
    for p in range(parts):
        grad_s[p] = grad[:, p * quarter : (p + 1) * quarter].astype(BF16)
    for p in range(parts):
        out_refs[p][...] = grad_s[(part_ref[0] + p) % parts]


def token_gradients(part, primal, tangent, layer_input, upstream, parts):
    tokens, width = layer_input.shape
    tile = 32
    quarter = width // parts
    spec = pl.BlockSpec((tile, width), lambda n, part: (n, 0))
    return pl.pallas_call(
        token_kernel,
        grid_spec=pltpu.PrefetchScalarGridSpec(
            num_scalar_prefetch=1,
            grid=(tokens // tile,),
            in_specs=[spec] * SIDE
            + [pl.BlockSpec((SIDE, tile, width), lambda n, part: (0, n, 0)), spec, spec],
            out_specs=[pl.BlockSpec((tile, quarter), lambda n, part: (n, 0))] * parts,
            scratch_shapes=[pltpu.VMEM((parts, tile, quarter), BF16)],
        ),
        out_shape=[jax.ShapeDtypeStruct((tokens, quarter), BF16)] * parts,
        compiler_params=params(),
    )(part, *primal, tangent, layer_input, upstream)


def turn_kernel(hidden_ref, out_ref):
    _, groups, cap, width = hidden_ref.shape
    out_ref[0, 0] = hidden_ref[0].reshape(groups * cap, width).T


def turned(hidden, local):
    parts, groups, slots, width = hidden.shape
    return pl.pallas_call(
        turn_kernel,
        grid=(parts, local),
        in_specs=[pl.BlockSpec((1, groups, CAP, width), lambda g, l: (g, 0, l, 0))],
        out_specs=pl.BlockSpec((1, 1, width, groups * CAP), lambda g, l: (g, l, 0, 0)),
        out_shape=jax.ShapeDtypeStruct((parts, local, width, groups * CAP), BF16),
        cost_estimate=pl.CostEstimate(
            flops=0, bytes_accessed=4 * hidden.size, transcendentals=0
        ),
        compiler_params=params(),
    )(hidden)


def estimate_kernel(
    part_ref, rank_ref, weight_ref, hidden_ref, grad_ref, probe_ref, out_ref, rows_s, total_s
):
    step = pl.program_id(0)
    groups, _, tokens, quarter = grad_ref.shape
    local = total_s.shape[0]
    steps = pl.num_programs(0) - local
    slots = local * CAP
    nothing = jnp.zeros((slots, tokens), BF16)

    @pl.when(step == 0)
    def _():
        total_s[...] = jnp.zeros(total_s.shape, F32)

    @pl.when(step < steps)
    def _():
        for i in range(0, groups, 2):
            high0, low0 = split_high_low(selection(rank_ref[0, i], weight_ref[0, i]))
            high1, low1 = split_high_low(selection(rank_ref[0, i + 1], weight_ref[0, i + 1]))
            first = jnp.concatenate([high0, nothing, low0, nothing], axis=0)
            second = jnp.concatenate([nothing, high1, nothing, low1], axis=0)
            sel = jnp.concatenate([first, second], axis=1)
            grads = grad_ref[i : i + 2, 0].reshape(2 * tokens, quarter)
            both = dot(sel, grads, ((1,), (0,)))
            rows = (both[: 2 * slots] + both[2 * slots :]).astype(BF16)
            for j in range(2):
                for l in range(local):
                    start = j * slots + l * CAP
                    rows_s[l, (i + j) * CAP : (i + j + 1) * CAP, :] = rows[start : start + CAP]

        for l in range(local):
            total_s[l] += dot(hidden_ref[0, l], rows_s[l], ((1,), (0,)))

    @pl.when(step >= steps)
    def _():
        out_ref[0] = total_s[step - steps] * probe_ref[0].astype(F32)


def estimate(part, rank, weight, hidden, grads, probe):
    parts, local, width_f, slots = hidden.shape
    groups, _, tokens, quarter = grads.shape

    def group(s, part):
        return (part[0] + parts - jnp.minimum(s, parts - 1)) % parts

    def expert(s):
        return jnp.maximum(s - parts, 0)

    routes = pl.BlockSpec((1, groups, local, tokens), lambda s, p: (group(s, p), 0, 0, 0))
    return pl.pallas_call(
        estimate_kernel,
        grid_spec=pltpu.PrefetchScalarGridSpec(
            num_scalar_prefetch=1,
            grid=(parts + local,),
            in_specs=[
                routes,
                routes,
                pl.BlockSpec((1, local, width_f, slots), lambda s, p: (group(s, p), 0, 0, 0)),
                pl.BlockSpec(
                    (groups, 1, tokens, quarter), lambda s, p: (0, jnp.minimum(s, parts - 1), 0, 0)
                ),
                pl.BlockSpec((1, width_f, quarter), lambda s, p: (expert(s), 0, p[0])),
            ],
            out_specs=pl.BlockSpec((1, width_f, quarter), lambda s, p: (expert(s), 0, 0)),
            scratch_shapes=[
                pltpu.VMEM((local, slots, quarter), BF16),
                pltpu.VMEM((local, width_f, quarter), F32),
            ],
        ),
        out_shape=jax.ShapeDtypeStruct((local, width_f, quarter), F32),
        cost_estimate=pl.CostEstimate(
            flops=2 * parts * slots * local * width_f * quarter,
            bytes_accessed=2 * (hidden.size + grads.size) + 6 * local * width_f * quarter,
            transcendentals=0,
        ),
        compiler_params=params(),
    )(part, rank, weight, hidden, grads, probe)


def routes_to(experts, ids, weights):
    tokens = ids.shape[-1]
    match = ids[:, None, :, :] == experts[..., :, None, None]
    named = jnp.any(match, axis=2)
    weight = jnp.sum(jnp.where(match, weights[:, None, :, :], 0.0), axis=2)
    before = jnp.triu(jnp.ones((tokens, tokens), F32), 1).astype(BF16)
    earlier = jnp.einsum("blt,tu->blu", named.astype(BF16), before, preferred_element_type=F32)
    return jnp.where(named, earlier.astype(jnp.int32), -1), weight


def shards(layer_input, upstream, hidden, route_ids, route_prob, down_weight, probe_signs):
    tokens, top = route_ids.shape
    local, width_f, width_d = down_weight.shape
    groups, parts = lax.axis_size("expert"), lax.axis_size("dp")
    experts = local * groups
    me, part = lax.axis_index("expert"), lax.axis_index("dp")
    x, y, core = me // (SIDE * CORES), me // CORES % SIDE, me % CORES
    side, cores = jnp.arange(SIDE, dtype=jnp.int32), jnp.arange(CORES, dtype=jnp.int32)

    combine = route_prob / jnp.sum(route_prob, axis=1, keepdims=True)
    facts = jnp.concatenate([route_ids.T.astype(F32), combine.T], axis=0)
    lines = [facts] + [shift(facts, 0, i, 0) for i in range(1, SIDE)]
    lines += [facts] + [shift(facts, i, 0, 0) for i in range(1, SIDE)]
    outgoing = place_routes(route_ids.reshape(1, -1), hidden.reshape(-1, width_f), experts)
    arrived = lax.all_to_all(
        outgoing.reshape(groups, local * CAP, -1), "expert", 0, 0, tiled=True
    )

    arrived, *lines[:-1] = lax.optimization_barrier((arrived, *lines[:-1]))

    order = device_at(
        side[:, None, None], side[None, None, :], cores[None, :, None]
    ).reshape(-1)
    (rows,) = expert_rows(order, arrived, probe_signs, 1)
    rows, lines[-1] = lax.optimization_barrier((rows, lines[-1]))
    along_x = [
        [device_at(i, j, c) for i in range(SIDE) for c in range(CORES)] for j in range(SIDE)
    ]
    tangent_rows = lax.all_to_all(
        rows.reshape(SIDE * CORES, SIDE, local * CAP, -1),
        "expert",
        0,
        0,
        axis_index_groups=along_x,
        tiled=True,
    )
    order = device_at(
        (x + side)[None, None, :] % SIDE,
        (y + side)[:, None, None] % SIDE,
        (core ^ cores)[None, :, None],
    ).reshape(-1)
    rows = expert_rows(order, arrived, down_weight, SIDE * CORES)
    primal_rows = [rows[0]]
    primal_rows += [
        shift(rows[i], 0, i // CORES, i % CORES) for i in range(1, SIDE * CORES)
    ]
    arrived_all = lax.all_gather(arrived, "dp", axis=0, tiled=False)
    hidden_all = turned(arrived_all, local)

    steps = jnp.concatenate([(y - side) % SIDE, SIDE + -side % SIDE])
    chosen = jnp.take(jnp.stack(lines), steps, axis=0)
    devices = jnp.stack(
        [
            device_at(side[:, None], y, cores[None, :]).reshape(-1),
            device_at(x, (y - side[:, None]) % SIDE, core ^ cores[None, :]).reshape(-1),
        ]
    )
    listed = (devices[:, :, None] * local + jnp.arange(local, dtype=jnp.int32)).reshape(2, -1)
    rank, weight = routes_to(
        jnp.repeat(listed, SIDE, axis=0), chosen[:, :top].astype(jnp.int32), chosen[:, top:]
    )
    rank, weight = (a.reshape(2, SIDE, -1, tokens) for a in (rank, weight))

    tangent_rows, *primal_rows = lax.optimization_barrier((tangent_rows, *primal_rows))
    sums, *primal = middle_sums(rank, weight, tangent_rows, primal_rows)
    along_y = [[device_at(i, j, c) for j in range(SIDE)] for i in range(SIDE) for c in range(CORES)]
    tangent = lax.all_to_all(sums, "expert", 0, 0, axis_index_groups=along_y, tiled=True)
    primal = [primal[0]] + [shift(primal[i], i, 0, 0) for i in range(1, SIDE)]
    tangent, hidden_all = lax.optimization_barrier((tangent, hidden_all))

    part_row = part.astype(jnp.int32).reshape(1)
    grads = token_gradients(part_row, primal, tangent, layer_input, upstream, parts)
    grads = [grads[0]] + [
        lax.ppermute(grads[i], "dp", [(j, (j + i) % parts) for j in range(parts)])
        for i in range(1, parts)
    ]
    high = lax.reduce_precision(combine, 8, 7)
    routes = jnp.concatenate([route_ids.astype(F32), high, combine - high], axis=1).T.astype(BF16)
    routes, grads = lax.optimization_barrier((routes, jnp.stack(grads)))
    grads_all = lax.all_gather(grads, "expert", axis=0, tiled=False)
    routes = lax.all_gather(routes, ("dp", "expert"), axis=0, tiled=False)
    ids = routes[:, :top].astype(jnp.int32)
    weights = routes[:, top : 2 * top].astype(F32) + routes[:, 2 * top :].astype(F32)
    own = me * local + jnp.arange(local, dtype=jnp.int32)
    rank, weight = routes_to(own, ids, weights)
    rank = rank.reshape(parts, groups, local, tokens)
    weight = weight.reshape(parts, groups, local, tokens)
    return estimate(part_row, rank, weight, hidden_all, grads_all, probe_signs)


def solution(mesh):
    in_specs = (
        P(("dp", "expert"), None),
        P(("dp", "expert"), None),
        P(("dp", "expert"), None, None),
        P(("dp", "expert"), None),
        P(("dp", "expert"), None),
        P("expert", None, None),
        P("expert", None, None),
    )
    out_specs = P("expert", None, "dp")
    return jax.shard_map(shards, mesh=mesh, in_specs=in_specs, out_specs=out_specs, check_vma=False)
```
